512 devices in a mesh: section: 2 (over x_hi), lat: 16 (over x_lo, y), lon: 16 (over z, core).
Axes of the slice: x: 4 (x_hi: 2, x_lo: 2; x = x_hi * 2 + x_lo), y: 8, z: 8, core: 2. Of those that a mesh axis runs over, the one named last changes fastest.
Arguments:
- fields_in: bfloat16 [4, 96, 256, 2048], P('section', None, 'lat', 'lon'), may hold values from -6 to 6
- plan: int32 [4], replicated, may hold values from 0 to 3, as said below
- in_proj: bfloat16 [64, 96], replicated, may hold values from -0.625 to 0.625
- enc_conv: bfloat16 [9, 64, 64], replicated, may hold values from -0.25 to 0.25
- down_conv: bfloat16 [9, 128, 64], replicated, may hold values from -0.25 to 0.25
- mid_conv: bfloat16 [9, 128, 128], replicated, may hold values from -0.1875 to 0.1875
- up_proj: bfloat16 [64, 128], replicated, may hold values from -0.5 to 0.5
- unite_conv: bfloat16 [9, 64, 128], replicated, may hold values from -0.1875 to 0.1875
- out_proj: bfloat16 [96, 64], replicated, may hold values from -0.75 to 0.75
Outputs:
- corrected: bfloat16 [4, 96, 256, 2048], P('section', None, 'lat', 'lon')
The draws below stay inside these ranges and needn't reach their ends.
Inputs may be any that keep to these rules, and one draw needn't show every extreme that they name: `plan`: each micro-batch appears once; the first turn takes one of the last 2 micro-batches and the last turn one of the first 2.
All inputs are finite; a program needn't handle non-finite values.
Results may differ from the reference program's by a relative error of at most 0.0072.
Values may be sent and summed in bfloat16 or wider, within the bound.
A program may use at most 64 MiB of HBM per device.

```python
import jax
import jax.numpy as jnp
from jax import lax

VARS = 96
C0 = 64
C1 = 128
MICRO = 4
LAT = 256
LON = 2048


def draw_plan(key, part):
    half_count = MICRO // 2
    opening = jax.random.randint(jax.random.fold_in(key, 11), (), half_count, MICRO).astype(jnp.int32)
    closing = jax.random.randint(jax.random.fold_in(key, 12), (), 0, half_count).astype(jnp.int32)
    shuffled = jax.random.permutation(jax.random.fold_in(key, 13), MICRO).astype(jnp.int32)
    position = jnp.argsort(shuffled, stable=True).astype(jnp.int32)
    numbers = jnp.arange(MICRO, dtype=jnp.int32)
    taken = (numbers == opening) | (numbers == closing)
    scores = jnp.where(taken, jnp.int32(2 * MICRO), position)
    remaining = jnp.argsort(scores, stable=True).astype(jnp.int32)[:MICRO - 2]
    return jnp.concatenate([opening[None], remaining, closing[None]]).astype(jnp.int32)


def block_levels(rng, dims, pieces, low, largest):
    gain = 1.0
    for dim, blocks in pieces:
        steps = jax.random.uniform(jax.random.fold_in(jax.random.fold_in(rng, 6), dim), (blocks,), jnp.float32, low / len(pieces), largest / len(pieces))
        gain = gain * jnp.repeat(jnp.exp(steps), dims[dim] // blocks).reshape((-1,) + (1,) * (len(dims) - 1 - dim))
    return gain


def centred(key, shape, deviation, reach, split=(), held_as=jnp.bfloat16):
    factor_of = block_levels(key, shape, split, -0.22, 0.18) if split else 1.0
    values = jax.random.normal(key, shape, jnp.float32) * deviation * factor_of
    return jnp.minimum(jnp.maximum(values, -reach), reach).astype(held_as)


def setup_inputs(seed: int = 0) -> dict:
    keys = jax.random.split(jax.random.key(seed), 10)
    fields_in = centred(keys[0], (MICRO, VARS, LAT, LON), 1.0, 6.0, ((0, 2), (2, 16), (3, 16)))
    plan = draw_plan(jax.random.fold_in(keys[9], 71), 0)
    in_proj = centred(keys[2], (C0, VARS), VARS ** -0.5, 0.625)
    enc_conv = centred(keys[3], (9, C0, C0), (9 * C0) ** -0.5, 0.25)
    down_conv = centred(keys[4], (9, C1, C0), (9 * C0) ** -0.5, 0.25)
    mid_conv = centred(keys[5], (9, C1, C1), (9 * C1) ** -0.5, 0.1875)
    up_proj = centred(keys[6], (C0, C1), C1 ** -0.5, 0.5)
    unite_conv = centred(keys[7], (9, C0, 2 * C0), (18 * C0) ** -0.5, 0.1875)
    out_proj = centred(keys[8], (VARS, C0), C0 ** -0.5, 0.75)
    return {"fields_in": fields_in, "plan": plan, "in_proj": in_proj, "enc_conv": enc_conv, "down_conv": down_conv, "mid_conv": mid_conv, "up_proj": up_proj, "unite_conv": unite_conv, "out_proj": out_proj}


def convolve(source, kernel):
    channels, height, breadth = source.shape
    padded = jnp.pad(source, ((0, 0), (0, 0), (1, 1)), mode="wrap")
    padded = jnp.pad(padded, ((0, 0), (1, 1), (0, 0)))
    summed = jnp.zeros((kernel.shape[1], height * breadth), jnp.float32)
    for offset_row in range(3):
        for offset_col in range(3):
            window = padded[:, offset_row:offset_row + height, offset_col:offset_col + breadth].reshape(channels, height * breadth)
            summed = summed + jnp.dot(kernel[3 * offset_row + offset_col], window, preferred_element_type=jnp.float32)
    return summed.reshape(kernel.shape[1], height, breadth)


def encode(sample, in_proj, enc_conv, down_conv):
    variables, height, breadth = sample.shape
    stem_map = jax.nn.gelu(jnp.dot(in_proj, sample.reshape(variables, height * breadth), preferred_element_type=jnp.float32))
    stem_map = stem_map.astype(jnp.bfloat16).reshape(-1, height, breadth)
    skip_map = jax.nn.gelu(convolve(stem_map, enc_conv)).astype(jnp.bfloat16)
    pooled = skip_map.astype(jnp.float32).reshape(-1, height // 2, 2, breadth // 2, 2).mean(axis=(2, 4)).astype(jnp.bfloat16)
    deep_map = jax.nn.gelu(convolve(pooled, down_conv)).astype(jnp.bfloat16)
    return skip_map, deep_map


def decode(skip_map, deep_map, mid_conv, up_proj, unite_conv, out_proj):
    middle = (jax.nn.gelu(convolve(deep_map, mid_conv)) + deep_map.astype(jnp.float32)).astype(jnp.bfloat16)
    wide_ch, half_h, half_w = middle.shape
    lifted = jnp.dot(up_proj, middle.reshape(wide_ch, half_h * half_w), preferred_element_type=jnp.float32)
    lifted = lifted.astype(jnp.bfloat16).reshape(-1, half_h, half_w)
    enlarged = jnp.repeat(jnp.repeat(lifted, 2, axis=1), 2, axis=2)
    joined = jnp.concatenate([enlarged, skip_map], axis=0)
    merged = jax.nn.gelu(convolve(joined, unite_conv)).astype(jnp.bfloat16)
    narrow_ch, height, breadth = merged.shape
    result = jnp.dot(out_proj, merged.reshape(narrow_ch, height * breadth), preferred_element_type=jnp.float32)
    return result.astype(jnp.bfloat16).reshape(-1, height, breadth)


def reference(fields_in, plan, in_proj, enc_conv, down_conv, mid_conv, up_proj, unite_conv, out_proj):
    results = []
    for tick_num in range(MICRO):
        sample = lax.dynamic_index_in_dim(fields_in, plan[tick_num].astype(jnp.int32), 0, keepdims=False)
        skip_map, deep_map = encode(sample, in_proj, enc_conv, down_conv)
        results.append(decode(skip_map, deep_map, mid_conv, up_proj, unite_conv, out_proj))
    return jnp.stack(results)
```

```python
import functools

import jax
import jax.numpy as jnp
from jax import lax
from jax.experimental import pallas as pl
from jax.experimental.pallas import tpu as pltpu
from jax.sharding import PartitionSpec as P

F32, BF = jnp.float32, jnp.bfloat16
MESH = pl.DeviceIdType.MESH

VARS, C0, C1 = 96, 64, 128
H, W = 16, 128
HP, WP = H // 2, W // 2
EXT = WP + 16
PADDED = EXT + 16
MID = slice(8, 8 + EXT)
PREV = slice(7, 7 + EXT)
NEXT = slice(9, 9 + EXT)
OWN = slice(16, 16 + WP)
OWN_PREV = slice(15, 15 + WP)
OWN_NEXT = slice(17, 17 + WP)


def gelu(x):
    half = 0.5 * x
    inner = x * (0.7978845608028654 + 0.035677408136300125 * (x * x))
    return half + half * jnp.tanh(inner)


def rounded(x):
    return x.astype(BF).astype(F32)


def nn(a, b):
    return jnp.dot(a, b, preferred_element_type=F32)


def nt(a, b):
    return lax.dot_general(a, b, (((1,), (1,)), ((), ())), preferred_element_type=F32)


def grid_iota(rows, cols):
    shape = (rows, cols)
    return lax.broadcasted_iota(jnp.int32, shape, 0), lax.broadcasted_iota(jnp.int32, shape, 1)


def one_hot(mask):
    return jnp.where(mask, 1.0, 0.0).astype(BF)


def eye(n):
    i, j = grid_iota(n, n)
    return one_hot(i == j)


def upper_lanes(rows):
    return lax.broadcasted_iota(jnp.int32, (rows, 128), 1) >= 64


def column_pairs(taps, channels):
    zero = jnp.zeros((C0, channels), BF)
    unit = eye(channels)
    out = []
    for a in range(3):
        b0, b1, b2 = taps[3 * a], taps[3 * a + 1], taps[3 * a + 2]
        stacked = jnp.concatenate([zero, b2, b1, b0, b2, b1, b0, zero], axis=0)
        out.append(nt(unit, stacked).astype(BF))
    return out


def fill_full_res(w_ref, base, blocks, rows):
    for k in range(4):
        for dr in range(2):
            a = k - dr
            lanes = slice(dr * 128, dr * 128 + 128)
            for at, col in ((0, 1), (64, 2), (512, 3), (576, 0)):
                where = base + at + k * 128
                if 0 <= a <= 2:
                    val = blocks[a][rows, col * 128 : col * 128 + 128]
                else:
                    val = jnp.zeros((64, 128), BF)
                w_ref[where : where + 64, lanes] = val


def prepare_enc(wenc, we):
    fill_full_res(we, 0, column_pairs(wenc, C0), slice(0, 64))


def prepare_down(wdown, wd):
    taps = nt(eye(C0), wdown[...].reshape(9 * C1, C0)).astype(BF)
    for k in range(4):
        for dr in range(2):
            a = k - dr
            for at, b in ((0, 0), (64, 2), (128, 1), (192, None)):
                where = k * 256 + at
                if b is not None and 0 <= a <= 2:
                    t = 3 * a + b
                    val = taps[:, t * 128 : t * 128 + 128]
                else:
                    val = jnp.zeros((64, 128), BF)
                wd[where : where + 64, dr * 128 : dr * 128 + 128] = val


def prepare_mid(wmid, wm):
    taps = nt(eye(C1), wmid[...].reshape(9 * C1, C1)).astype(BF)
    for k in range(4):
        for dr in range(2):
            a = k - dr
            for b in range(3):
                where = k * 384 + b * 128
                if 0 <= a <= 2:
                    t = 3 * a + b
                    val = taps[:, t * 128 : t * 128 + 128]
                else:
                    val = jnp.zeros((128, 128), BF)
                wm[where : where + 128, dr * 128 : dr * 128 + 128] = val


def prepare_unite(wun, wu):
    blocks = column_pairs(wun, 2 * C0)
    fill_full_res(wu, 0, blocks, slice(64, 128))
    fill_full_res(wu, 1024, blocks, slice(0, 64))


def stem_rows(x_ref, index, win_ref, fx, dest):
    fx[...] = x_ref[index].astype(F32).reshape(VARS * H, W)
    i, j = grid_iota(128, 128)
    spread = one_hot(j == 2 * (i % 64) + i // 64)
    win = win_ref[...]
    hi = upper_lanes(WP)

    def body(g, carry):
        rows = [fx[pl.ds(4 * g + k, VARS, stride=H), :].astype(BF) for k in range(4)]
        y = gelu(nn(win, jnp.concatenate(rows, axis=1))).astype(BF)
        stacked = jnp.concatenate([y[:, k * W : k * W + W] for k in range(4)], axis=0)
        z = nt(spread, stacked)
        for k in range(2):
            even = z[:WP, k * 128 : k * 128 + 128]
            odd = z[WP:, k * 128 : k * 128 + 128]
            dest[4 * g + 2 * k] = jnp.where(hi, pltpu.roll(odd, 64, 1), even).astype(BF)
            dest[4 * g + 2 * k + 1] = jnp.where(hi, odd, pltpu.roll(even, 64, 1)).astype(BF)
        return carry

    lax.fori_loop(0, H // 4, body, 0)


def edge_columns(main, low, high):
    def body(q, carry):
        r0, r1 = main.at[2 * q], main.at[2 * q + 1]
        low[q] = jnp.concatenate(
            [r0[0:16].astype(F32)[0:8], r1[0:16].astype(F32)[0:8]], axis=0
        ).astype(BF)
        high[q] = jnp.concatenate(
            [r0[48:64].astype(F32)[8:16], r1[48:64].astype(F32)[8:16]], axis=0
        ).astype(BF)
        return carry

    lax.fori_loop(0, HP, body, 0)


def widened(main, halo, f, ee, eb):
    top, bot, left, right, ctl, ctr, cbl, cbr = halo

    def sides(q, at, lref, rref):
        lv, rv = lref[q].astype(F32), rref[q].astype(F32)
        f[at, 8:16] = lv[0:8]
        f[at + 1, 8:16] = lv[8:16]
        f[at, 80:88] = rv[0:8]
        f[at + 1, 80:88] = rv[8:16]

    def own(q, carry):
        sides(q, 8 + 2 * q, left, right)
        f[8 + 2 * q, OWN] = main[2 * q].astype(F32)
        f[9 + 2 * q, OWN] = main[2 * q + 1].astype(F32)
        return carry

    def corner(q, carry):
        sides(q, 2 * q, ctl, ctr)
        sides(q, 24 + 2 * q, cbl, cbr)
        return carry

    def rims(t, carry):
        f[1 + t, OWN] = top[t].astype(F32)
        f[24 + t, OWN] = bot[t].astype(F32)
        return carry

    lax.fori_loop(0, HP, own, 0)
    lax.fori_loop(0, 4, corner, 0)
    lax.fori_loop(0, 7, rims, 0)
    hi = upper_lanes(EXT)

    def split(q, carry):
        for par in range(2):
            rr = 2 * q + par
            ee[par, q] = f[rr, MID].astype(BF)
            eb[par, q] = pltpu.roll(jnp.where(hi, f[rr, PREV], f[rr, NEXT]), 64, 1).astype(BF)
        return carry

    lax.fori_loop(0, 16, split, 0)


def quads(refs, first, count):
    pieces = []
    for ref in refs:
        for par, lag in ((1, 0), (0, 1), (1, 1), (0, 2)):
            v = ref[par, pl.ds(first + lag, count)]
            pieces.append(v.reshape(-1, v.shape[-1]))
    return jnp.concatenate(pieces, axis=1)


def kept(value, keep):
    return jnp.where(keep, value, 0.0)


def encoder(above, below, ee, eb, we, fs, fp, qc, qs, group):
    def body(g, carry):
        first = g * group
        y = rounded(gelu(nn(quads((ee, eb), first, group), we[...])))
        for p in range(group):
            ii = first + p
            keep = ((ii >= 3) | above) & ((ii <= 10) | below)
            v = kept(y[p * EXT : p * EXT + EXT], keep)
            v0, v1 = v[:, :128], v[:, 128:]
            fs[2 * ii, MID] = v0
            fs[2 * ii + 1, MID] = v1
            s = v0 + v1
            fp[ii, MID] = rounded((s + pltpu.roll(s, 64, 1)) * 0.25)
        return carry

    lax.fori_loop(0, 14 // group, body, 0)
    hi = upper_lanes(EXT)

    def split(q, carry):
        for par in range(2):
            ii = 2 * q + par
            qc[par, q] = fp[ii, MID].astype(BF)
            qs[par, q] = jnp.where(hi, fp[ii, NEXT], fp[ii, PREV]).astype(BF)
        return carry

    lax.fori_loop(0, 7, split, 0)


def row_quads(refs, first, count):
    pieces = []
    for lag in range(2):
        for par in range(2):
            for ref in refs:
                v = ref[par, pl.ds(first + lag, count)]
                pieces.append(v.reshape(-1, v.shape[-1]))
    return jnp.concatenate(pieces, axis=1)


def deepest(above, below, qc, qs, wd, wm, wup_ref, fd, dm, dc, dp, fl, group_d, group_m):
    def down(g, carry):
        first = g * group_d
        y = rounded(gelu(nn(row_quads((qs, qc), first, group_d), wd[...])))
        for p in range(group_d):
            k = first + p
            keep = ((k >= 1) | above) & ((k <= 4) | below)
            v = kept(y[p * EXT : p * EXT + EXT], keep)
            fd[2 * k, MID] = v[:, :128]
            fd[2 * k + 1, MID] = v[:, 128:]
        return carry

    lax.fori_loop(0, 6 // group_d, down, 0)

    def split(q, carry):
        for par in range(2):
            dd = 2 * q + par
            dm[par, q] = fd[dd, PREV].astype(BF)
            dc[par, q] = fd[dd, MID].astype(BF)
            dp[par, q] = fd[dd, NEXT].astype(BF)
        return carry

    lax.fori_loop(0, 6, split, 0)
    up = jnp.concatenate([wup_ref[...], wup_ref[...]], axis=0)

    def mid(g, carry):
        first = g * group_m
        y = gelu(nn(row_quads((dm, dc, dp), first, group_m), wm[...]))
        rows = []
        for p in range(group_m):
            k = first + p
            for dr in range(2):
                v = y[p * EXT : p * EXT + EXT, dr * 128 : dr * 128 + 128]
                v = v + fd[2 * k + 1 + dr, MID]
                if dr == 0:
                    keep = (k >= 1) | above
                else:
                    keep = (k <= 3) | below
                rows.append(kept(v, keep).astype(BF))
        z = rounded(nt(jnp.concatenate(rows, axis=0), up))
        for p in range(group_m):
            k = first + p
            for dr in range(2):
                at = (2 * p + dr) * EXT
                fl[2 * k + dr, MID] = z[at : at + EXT]
        return carry

    lax.fori_loop(0, 5 // group_m, mid, 0)


def join_operands(fs, fl, sc, sb, lc, lb):
    hi = upper_lanes(WP)

    def skip(q, carry):
        for par in range(2):
            idx = 2 * (q + 2) + par
            sc[par, q] = fs[idx, OWN].astype(BF)
            sb[par, q] = pltpu.roll(
                jnp.where(hi, fs[idx, OWN_PREV], fs[idx, OWN_NEXT]), 64, 1
            ).astype(BF)
        return carry

    lax.fori_loop(0, 10, skip, 0)

    def lift(m, carry):
        lc[m] = fl[m, OWN].astype(BF)
        lb[m] = jnp.where(hi, fl[m, OWN_NEXT], fl[m, OWN_PREV]).astype(BF)
        return carry

    lax.fori_loop(0, 10, lift, 0)


def unite(sc, sb, lc, lb, wu, first, group):
    pieces = [quads((sc, sb), first, group)]
    for ref in (lc, lb):
        for lag in (0, 1, 1, 2):
            pieces.append(ref[pl.ds(first + lag, group)].reshape(-1, 128))
    return gelu(nn(jnp.concatenate(pieces, axis=1), wu[...])).astype(BF)


def kernel(
    plan, x_ref, win, wenc, wdown, wmid, wup, wun, out_ref,
    fx, send_a, main_b, recv_a, low, high, top, bot, left, right, ctl, ctr, cbl, cbr,
    f, ee, eb, fs, fp, qc, qs, fd, dm, dc, dp, fl, sc, sb, lc, lb,
    merged_b, recv_b, we, wd, wm, wu,
    halo_send, halo_recv, a_send, a_recv, b_send, b_recv,
):
    section, lat, lon = lax.axis_index("section"), lax.axis_index("lat"), lax.axis_index("lon")
    lats, lons = lax.axis_size("lat"), lax.axis_size("lon")
    above, below = lat > 0, lat < lats - 1
    up, dn = jnp.maximum(lat - 1, 0), jnp.minimum(lat + 1, lats - 1)
    lt, rt = lax.rem(lon + lons - 1, lons), lax.rem(lon + 1, lons)
    partner = (1 - section, lat, lon)

    barrier = pltpu.get_barrier_semaphore()

    def greet(device):
        pl.semaphore_signal(barrier, inc=1, device_id=device, device_id_type=MESH)

    greet(partner)
    greet((section, lat, lt))
    greet((section, lat, rt))

    @pl.when(above)
    def _():
        for c in (lt, lon, rt):
            greet((section, up, c))

    @pl.when(below)
    def _():
        for c in (lt, lon, rt):
            greet((section, dn, c))

    index_a = lax.rem(jnp.where(section == 1, plan[0], plan[3]), 2)
    stem_rows(x_ref, index_a, win, fx, send_a)

    pl.semaphore_wait(barrier, 3 + jnp.where(above, 3, 0) + jnp.where(below, 3, 0))

    copy_a = pltpu.make_async_remote_copy(
        src_ref=send_a, dst_ref=recv_a, send_sem=a_send, recv_sem=a_recv,
        device_id=partner, device_id_type=MESH,
    )
    copy_a.start()

    def halo_copies(n, main):
        def rc(d, src, dst, device):
            return pltpu.make_async_remote_copy(
                src_ref=src, dst_ref=dst, send_sem=halo_send.at[n, d], recv_sem=halo_recv.at[n, d],
                device_id=device, device_id_type=MESH,
            )

        lo, hi = low.at[n], high.at[n]
        upward = [
            rc(0, main.at[0:7], bot.at[n], (section, up, lon)),
            rc(1, lo.at[0:4], cbr.at[n], (section, up, lt)),
            rc(2, hi.at[0:4], cbl.at[n], (section, up, rt)),
        ]
        downward = [
            rc(3, main.at[9:16], top.at[n], (section, dn, lon)),
            rc(4, lo.at[4:8], ctr.at[n], (section, dn, lt)),
            rc(5, hi.at[4:8], ctl.at[n], (section, dn, rt)),
        ]
        across = [
            rc(6, lo, right.at[n], (section, lat, lt)),
            rc(7, hi, left.at[n], (section, lat, rt)),
        ]
        return upward, downward, across

    def start_halo(n, main):
        edge_columns(main, low.at[n], high.at[n])
        upward, downward, across = halo_copies(n, main)

        @pl.when(above)
        def _():
            for c in upward:
                c.start()

        @pl.when(below)
        def _():
            for c in downward:
                c.start()

        for c in across:
            c.start()

        @pl.when(jnp.logical_not(above))
        def _():
            for ref in (top, ctl, ctr):
                ref[n] = jnp.zeros(ref.shape[1:], BF)

        @pl.when(jnp.logical_not(below))
        def _():
            for ref in (bot, cbl, cbr):
                ref[n] = jnp.zeros(ref.shape[1:], BF)

    def finish_halo(n, main):
        upward, downward, across = halo_copies(n, main)

        @pl.when(above)
        def _():
            for c in upward:
                c.wait_send()
            for c in downward:
                c.wait_recv()

        @pl.when(below)
        def _():
            for c in downward:
                c.wait_send()
            for c in upward:
                c.wait_recv()

        for c in across:
            c.wait()

    def halo(n):
        return [r.at[n] for r in (top, bot, left, right, ctl, ctr, cbl, cbr)]

    stem_rows(x_ref, 1 - index_a, win, fx, main_b)
    start_halo(0, main_b)

    prepare_enc(wenc, we)
    prepare_down(wdown, wd)
    prepare_mid(wmid, wm)
    prepare_unite(wun, wu)
    for ref in (f, fs, fp, fd, fl):
        rows = ref.shape[0]
        ref[:, 0:8] = jnp.zeros((rows, 8, 128), F32)
        ref[:, PADDED - 8 :] = jnp.zeros((rows, 8, 128), F32)

    finish_halo(0, main_b)
    widened(main_b, halo(0), f, ee, eb)
    encoder(above, below, ee, eb, we, fs, fp, qc, qs, 2)
    deepest(above, below, qc, qs, wd, wm, wup, fd, dm, dc, dp, fl, 2, 1)

    copy_a.wait()
    start_halo(1, recv_a)

    join_operands(fs, fl, sc, sb, lc, lb)

    def copy_b(g):
        rows = pl.ds(g * 2, 2)
        return pltpu.make_async_remote_copy(
            src_ref=merged_b.at[rows], dst_ref=recv_b.at[rows],
            send_sem=b_send.at[g], recv_sem=b_recv.at[g],
            device_id=partner, device_id_type=MESH,
        )

    def unite_b(g, carry):
        merged_b[pl.ds(2 * g, 2)] = unite(sc, sb, lc, lb, wu, 2 * g, 2).reshape(2, WP, 256)
        copy_b(g).start()
        return carry

    lax.fori_loop(0, 4, unite_b, 0)

    finish_halo(1, recv_a)
    widened(recv_a, halo(1), f, ee, eb)
    encoder(above, below, ee, eb, we, fs, fp, qc, qs, 2)
    deepest(above, below, qc, qs, wd, wm, wup, fd, dm, dc, dp, fl, 2, 1)
    join_operands(fs, fl, sc, sb, lc, lb)

    def unite_a(g, carry):
        out_ref[section, pl.ds(2 * g, 2)] = unite(sc, sb, lc, lb, wu, 2 * g, 2).reshape(2, WP, 256)
        return carry

    lax.fori_loop(0, 4, unite_a, 0)

    for g in range(4):
        copy_b(g).wait()
    stays = jnp.where(section == 0, plan[1] < 2, plan[2] >= 2)

    def choose(i, carry):
        out_ref[1 - section, i] = jnp.where(stays, merged_b[i], recv_b[i])
        return carry

    lax.fori_loop(0, HP, choose, 0)


def project(m_ref, wout_ref, out_ref, fo):
    w = wout_ref[...]
    zero = jnp.zeros((VARS, C0), BF)
    both = jnp.concatenate(
        [jnp.concatenate([w, zero], axis=1), jnp.concatenate([zero, w], axis=1)], axis=0
    )
    i, j = grid_iota(256, 256)
    gather = one_hot((i // 64 % 2 == j // 128) & (j % 128 == 2 * (i % 64) + i // 128))
    for p in range(HP):
        m = m_ref[0, p]
        rows = jnp.concatenate([m[:, :128], m[:, 128:]], axis=0)
        u = nt(both, rows).astype(BF)
        v = nn(jnp.concatenate([u[:VARS], u[VARS:]], axis=1), gather)
        fo[pl.ds(2 * p, VARS, stride=H), :] = v[:, :128]
        fo[pl.ds(2 * p + 1, VARS, stride=H), :] = v[:, 128:]
    out_ref[0] = fo[...].reshape(VARS, H, W).astype(BF)


def shards(fields_in, plan, in_proj, enc_conv, down_conv, mid_conv, up_proj, unite_conv, out_proj):
    vmem = pl.BlockSpec(memory_space=pltpu.VMEM)
    dma = pltpu.SemaphoreType.DMA
    bf = lambda *s: pltpu.VMEM(s, BF)
    fl = lambda *s: pltpu.VMEM(s, F32)
    merged = pl.pallas_call(
        kernel,
        name="unet",
        out_shape=jax.ShapeDtypeStruct((2, HP, WP, 256), BF),
        in_specs=[pl.BlockSpec(memory_space=pltpu.SMEM)] + [vmem] * 7,
        out_specs=vmem,
        scratch_shapes=[
            fl(VARS * H, W),
            bf(H, WP, 128), bf(H, WP, 128), bf(H, WP, 128),
            bf(2, 8, 16, 128), bf(2, 8, 16, 128),
            bf(2, 7, WP, 128), bf(2, 7, WP, 128),
            bf(2, 8, 16, 128), bf(2, 8, 16, 128),
            bf(2, 4, 16, 128), bf(2, 4, 16, 128), bf(2, 4, 16, 128), bf(2, 4, 16, 128),
            fl(32, PADDED, 128), bf(2, 16, EXT, 128), bf(2, 16, EXT, 128),
            fl(28, PADDED, 128), fl(14, PADDED, 128), bf(2, 7, EXT, 128), bf(2, 7, EXT, 128),
            fl(12, PADDED, 128), bf(2, 6, EXT, 128), bf(2, 6, EXT, 128), bf(2, 6, EXT, 128),
            fl(10, PADDED, 128),
            bf(2, 10, WP, 128), bf(2, 10, WP, 128), bf(10, WP, 128), bf(10, WP, 128),
            bf(HP, WP, 256), bf(HP, WP, 256),
            bf(1024, 256), bf(1024, 256), bf(1536, 256), bf(2048, 256),
            dma((2, 8)), dma((2, 8)), dma, dma, dma((4,)), dma((4,)),
        ],
        compiler_params=pltpu.CompilerParams(
            collective_id=0, has_side_effects=True, vmem_limit_bytes=40 * 2**20
        ),
    )(plan, fields_in, in_proj, enc_conv, down_conv, mid_conv, up_proj, unite_conv)
    return pl.pallas_call(
        project,
        name="project",
        grid=(2,),
        out_shape=jax.ShapeDtypeStruct((2, VARS, H, W), BF),
        in_specs=[
            pl.BlockSpec((1, HP, WP, 256), lambda t: (t, 0, 0, 0)),
            pl.BlockSpec((VARS, C0), lambda t: (0, 0)),
        ],
        out_specs=pl.BlockSpec((1, VARS, H, W), lambda t: (t, 0, 0, 0)),
        scratch_shapes=[pltpu.VMEM((VARS * H, W), F32)],
    )(merged, out_proj)


def solution(mesh):
    return jax.shard_map(
        shards,
        mesh=mesh,
        in_specs=(P("section", None, "lat", "lon"), P(), P(), P(), P(), P(), P(), P(), P()),
        out_specs=P("section", None, "lat", "lon"),
        check_vma=False,
    )
```

```python
import functools

import jax
import jax.numpy as jnp
from jax import lax
from jax.experimental import pallas as pl
from jax.experimental.pallas import tpu as pltpu
from jax.sharding import PartitionSpec as P

F32, BF = jnp.float32, jnp.bfloat16
MESH = pl.DeviceIdType.MESH

VARS, C0, C1 = 96, 64, 128
H, W = 16, 128
HP, WP = H // 2, W // 2
EXT = WP + 16
PADDED = EXT + 16
MID = slice(8, 8 + EXT)
PREV = slice(7, 7 + EXT)
NEXT = slice(9, 9 + EXT)
OWN = slice(16, 16 + WP)
OWN_PREV = slice(15, 15 + WP)
OWN_NEXT = slice(17, 17 + WP)


def gelu(x):
    half = 0.5 * x
    inner = x * (0.7978845608028654 + 0.035677408136300125 * (x * x))
    return half + half * jnp.tanh(inner)


def rounded(x):
    return x.astype(BF).astype(F32)


def nn(a, b):
    return jnp.dot(a, b, preferred_element_type=F32)


def nt(a, b):
    return lax.dot_general(a, b, (((1,), (1,)), ((), ())), preferred_element_type=F32)


def grid_iota(rows, cols):
    shape = (rows, cols)
    return lax.broadcasted_iota(jnp.int32, shape, 0), lax.broadcasted_iota(jnp.int32, shape, 1)


def one_hot(mask):
    return jnp.where(mask, 1.0, 0.0).astype(BF)


def loop(count, step, body):
    def several(i, carry):
        for k in range(step):
            body(i * step + k)
        return carry

    if count == step:
        several(0, 0)
    else:
        lax.fori_loop(0, count // step, several, 0)


def eye(n):
    i, j = grid_iota(n, n)
    return one_hot(i == j)


def upper_lanes(rows):
    return lax.broadcasted_iota(jnp.int32, (rows, 128), 1) >= 64


def column_pairs(taps, channels):
    zero = jnp.zeros((C0, channels), BF)
    unit = eye(channels)
    out = []
    for a in range(3):
        b0, b1, b2 = taps[3 * a], taps[3 * a + 1], taps[3 * a + 2]
        stacked = jnp.concatenate([zero, b2, b1, b0, b2, b1, b0, zero], axis=0)
        out.append(nt(unit, stacked).astype(BF))
    return out


def fill_full_res(w_ref, base, blocks, rows):
    for k in range(4):
        for dr in range(2):
            a = k - dr
            lanes = slice(dr * 128, dr * 128 + 128)
            for at, col in ((0, 1), (64, 2), (512, 3), (576, 0)):
                where = base + at + k * 128
                if 0 <= a <= 2:
                    val = blocks[a][rows, col * 128 : col * 128 + 128]
                else:
                    val = jnp.zeros((64, 128), BF)
                w_ref[where : where + 64, lanes] = val


def prepare_enc(wenc, we):
    fill_full_res(we, 0, column_pairs(wenc, C0), slice(0, 64))


def prepare_down(wdown, wd):
    for k in range(4):
        for dr in range(2):
            a = k - dr
            for at, b in ((0, 0), (64, 2), (128, 1), (192, None)):
                where = k * 256 + at
                if b is not None and 0 <= a <= 2:
                    val = wdown[3 * a + b]
                else:
                    val = jnp.zeros((64, 128), BF)
                wd[where : where + 64, dr * 128 : dr * 128 + 128] = val


def prepare_mid(wmid, wm):
    taps = nt(eye(C1), wmid[...].reshape(9 * C1, C1)).astype(BF)
    for k in range(4):
        for dr in range(2):
            a = k - dr
            for b in range(3):
                where = k * 384 + b * 128
                if 0 <= a <= 2:
                    t = 3 * a + b
                    val = taps[:, t * 128 : t * 128 + 128]
                else:
                    val = jnp.zeros((128, 128), BF)
                wm[where : where + 128, dr * 128 : dr * 128 + 128] = val


def prepare_unite(wun, wu):
    blocks = column_pairs(wun, 2 * C0)
    fill_full_res(wu, 0, blocks, slice(64, 128))
    fill_full_res(wu, 1024, blocks, slice(0, 64))


def stem_rows(x_ref, index, win_ref, fx, dest, half):
    if half == 0:
        fx[...] = x_ref[index].astype(F32).reshape(VARS * H, W)
    i, j = grid_iota(128, 128)
    spread = one_hot(j == 2 * (i % 64) + i // 64)
    win = win_ref[...]
    hi = upper_lanes(WP)

    def body(g):
        first = 8 * half + 4 * g
        rows = [fx[pl.ds(first + k, VARS, stride=H), :].astype(BF) for k in range(4)]
        y = gelu(nn(win, jnp.concatenate(rows, axis=1))).astype(BF)
        stacked = jnp.concatenate([y[:, k * W : k * W + W] for k in range(4)], axis=0)
        z = nt(spread, stacked)
        for k in range(2):
            even = z[:WP, k * 128 : k * 128 + 128]
            odd = z[WP:, k * 128 : k * 128 + 128]
            at = first + 2 * k
            dest[at] = jnp.where(hi, pltpu.roll(odd, 64, 1), even).astype(BF)
            dest[at + 1] = jnp.where(hi, odd, pltpu.roll(even, 64, 1)).astype(BF)

    loop(2, 2, body)


def edge_columns(main, low, high, half):
    def body(k):
        q = 4 * half + k
        r0, r1 = main.at[2 * q], main.at[2 * q + 1]
        low[q] = jnp.concatenate(
            [r0[0:16].astype(F32)[0:8], r1[0:16].astype(F32)[0:8]], axis=0
        ).astype(BF)
        high[q] = jnp.concatenate(
            [r0[48:64].astype(F32)[8:16], r1[48:64].astype(F32)[8:16]], axis=0
        ).astype(BF)

    loop(4, 4, body)


def widened(main, halo, f, ee, eb):
    top, bot, left, right, ctl, ctr, cbl, cbr = halo

    def sides(q, at, lref, rref):
        lv, rv = lref[q].astype(F32), rref[q].astype(F32)
        f[at, 8:16] = lv[0:8]
        f[at + 1, 8:16] = lv[8:16]
        f[at, 80:88] = rv[0:8]
        f[at + 1, 80:88] = rv[8:16]

    def own(q):
        sides(q, 8 + 2 * q, left, right)
        f[8 + 2 * q, OWN] = main[2 * q].astype(F32)
        f[9 + 2 * q, OWN] = main[2 * q + 1].astype(F32)

    def corner(q):
        sides(q, 2 * q, ctl, ctr)
        sides(q, 24 + 2 * q, cbl, cbr)

    def rims(t):
        f[1 + t, OWN] = top[t].astype(F32)
        f[24 + t, OWN] = bot[t].astype(F32)

    loop(HP, 4, own)
    loop(4, 4, corner)
    loop(7, 7, rims)
    hi = upper_lanes(EXT)

    def split(q):
        for par in range(2):
            rr = 2 * q + par
            ee[par, q] = f[rr, MID].astype(BF)
            eb[par, q] = pltpu.roll(jnp.where(hi, f[rr, PREV], f[rr, NEXT]), 64, 1).astype(BF)

    loop(16, 4, split)


def quads(refs, first, count):
    pieces = []
    for ref in refs:
        for par, lag in ((1, 0), (0, 1), (1, 1), (0, 2)):
            v = ref[par, pl.ds(first + lag, count)]
            pieces.append(v.reshape(-1, v.shape[-1]))
    return jnp.concatenate(pieces, axis=1)


def kept(value, keep):
    return jnp.where(keep, value, 0.0)


def encoder(above, below, ee, eb, we, fs, fp, qc, qs, group):
    def body(g):
        first = g * group
        y = rounded(gelu(nn(quads((ee, eb), first, group), we[...])))
        for p in range(group):
            ii = first + p
            keep = ((ii >= 3) | above) & ((ii <= 10) | below)
            v = kept(y[p * EXT : p * EXT + EXT], keep)
            v0, v1 = v[:, :128], v[:, 128:]
            fs[2 * ii, MID] = v0
            fs[2 * ii + 1, MID] = v1
            s = v0 + v1
            fp[ii, MID] = rounded((s + pltpu.roll(s, 64, 1)) * 0.25)

    loop(14 // group, 1, body)
    hi = upper_lanes(EXT)

    def split(q):
        for par in range(2):
            ii = 2 * q + par
            qc[par, q] = fp[ii, MID].astype(BF)
            qs[par, q] = jnp.where(hi, fp[ii, NEXT], fp[ii, PREV]).astype(BF)

    loop(7, 7, split)


def row_quads(refs, first, count):
    pieces = []
    for lag in range(2):
        for par in range(2):
            for ref in refs:
                v = ref[par, pl.ds(first + lag, count)]
                pieces.append(v.reshape(-1, v.shape[-1]))
    return jnp.concatenate(pieces, axis=1)


def deepen(above, below, qc, qs, wd, fd, dm, dc, dp, group_d):
    def down(g):
        first = g * group_d
        y = rounded(gelu(nn(row_quads((qs, qc), first, group_d), wd[...])))
        for p in range(group_d):
            k = first + p
            keep = ((k >= 1) | above) & ((k <= 4) | below)
            v = kept(y[p * EXT : p * EXT + EXT], keep)
            fd[2 * k, MID] = v[:, :128]
            fd[2 * k + 1, MID] = v[:, 128:]

    loop(6 // group_d, 1, down)

    def split(q):
        for par in range(2):
            dd = 2 * q + par
            dm[par, q] = fd[dd, PREV].astype(BF)
            dc[par, q] = fd[dd, MID].astype(BF)
            dp[par, q] = fd[dd, NEXT].astype(BF)

    loop(6, 3, split)


def lift(above, below, dm, dc, dp, fd, wm, wup_ref, fl, group_m):
    up = jnp.concatenate([wup_ref[...], wup_ref[...]], axis=0)

    def mid(g):
        first = g * group_m
        y = gelu(nn(row_quads((dm, dc, dp), first, group_m), wm[...]))
        rows = []
        for p in range(group_m):
            k = first + p
            for dr in range(2):
                v = y[p * EXT : p * EXT + EXT, dr * 128 : dr * 128 + 128]
                v = v + fd[2 * k + 1 + dr, MID]
                if dr == 0:
                    keep = (k >= 1) | above
                else:
                    keep = (k <= 3) | below
                rows.append(kept(v, keep).astype(BF))
        z = rounded(nt(jnp.concatenate(rows, axis=0), up))
        for p in range(group_m):
            k = first + p
            for dr in range(2):
                at = (2 * p + dr) * EXT
                fl[2 * k + dr, MID] = z[at : at + EXT]

    loop(5 // group_m, 1, mid)


def join_operands(fs, fl, sc, sb, lc, lb):
    hi = upper_lanes(WP)

    def skip(q):
        for par in range(2):
            idx = 2 * (q + 2) + par
            sc[par, q] = fs[idx, OWN].astype(BF)
            sb[par, q] = pltpu.roll(
                jnp.where(hi, fs[idx, OWN_PREV], fs[idx, OWN_NEXT]), 64, 1
            ).astype(BF)

    loop(10, 5, skip)

    def lift(m):
        lc[m] = fl[m, OWN].astype(BF)
        lb[m] = jnp.where(hi, fl[m, OWN_NEXT], fl[m, OWN_PREV]).astype(BF)

    loop(10, 10, lift)


def unite(sc, sb, lc, lb, wu, first, group):
    pieces = [quads((sc, sb), first, group)]
    for ref in (lc, lb):
        for lag in (0, 1, 1, 2):
            pieces.append(ref[pl.ds(first + lag, group)].reshape(-1, 128))
    return gelu(nn(jnp.concatenate(pieces, axis=1), wu[...])).astype(BF)


def kernel(
    plan, x_hbm, win_hbm, wenc_hbm, wdown_hbm, wmid_hbm, wup_hbm, wun_hbm, out_hbm,
    x_ref, win, wenc, wdown, wmid, wup, wun,
    fx, send_a, main_b, recv_a, low, high, top, bot, left, right, ctl, ctr, cbl, cbr,
    f, ee, eb, fs, fp, qc, qs, fd, dm, dc, dp, fl, sc, sb, lc, lb,
    merged_a, merged_b, recv_b, we, wd, wm, wu,
    x_sem, w_sem, out_sem, halo_send, halo_recv, a_send, a_recv, b_send, b_recv,
):
    section, lat, lon = lax.axis_index("section"), lax.axis_index("lat"), lax.axis_index("lon")
    lats, lons = lax.axis_size("lat"), lax.axis_size("lon")
    above, below = lat > 0, lat < lats - 1
    up, dn = jnp.maximum(lat - 1, 0), jnp.minimum(lat + 1, lats - 1)
    lt, rt = lax.rem(lon + lons - 1, lons), lax.rem(lon + 1, lons)
    partner = (1 - section, lat, lon)

    loads_w = [
        pltpu.make_async_copy(src, dst, w_sem.at[n])
        for n, (src, dst) in enumerate(
            (
                (win_hbm, win),
                (wenc_hbm, wenc),
                (wdown_hbm, wdown),
                (wmid_hbm, wmid),
                (wup_hbm, wup),
                (wun_hbm, wun),
            )
        )
    ]
    loads_x = [
        pltpu.make_async_copy(
            x_hbm.at[n // 4, pl.ds(n % 4 * 24, 24)],
            x_ref.at[n // 4, pl.ds(n % 4 * 24, 24)],
            x_sem.at[n],
        )
        for n in range(8)
    ]
    loads_w[0].start()
    for c in loads_x:
        c.start()
    for c in loads_w[1:]:
        c.start()

    barrier = pltpu.get_barrier_semaphore()

    def greet(device):
        pl.semaphore_signal(barrier, inc=1, device_id=device, device_id_type=MESH)

    greet(partner)
    greet((section, lat, lt))
    greet((section, lat, rt))

    @pl.when(above)
    def _():
        for c in (lt, lon, rt):
            greet((section, up, c))

    @pl.when(below)
    def _():
        for c in (lt, lon, rt):
            greet((section, dn, c))

    def copy_a(half):
        rows = pl.ds(8 * half, 8)
        return pltpu.make_async_remote_copy(
            src_ref=send_a.at[rows], dst_ref=recv_a.at[rows],
            send_sem=a_send.at[half], recv_sem=a_recv.at[half],
            device_id=partner, device_id_type=MESH,
        )

    def copy_b(half):
        rows = pl.ds(4 * half, 4)
        return pltpu.make_async_remote_copy(
            src_ref=merged_b.at[rows], dst_ref=recv_b.at[rows],
            send_sem=b_send.at[half], recv_sem=b_recv.at[half],
            device_id=partner, device_id_type=MESH,
        )

    def halo_copies(n, main, half):
        def rc(d, src, dst, device):
            return pltpu.make_async_remote_copy(
                src_ref=src, dst_ref=dst,
                send_sem=halo_send.at[n, d + 5 * half], recv_sem=halo_recv.at[n, d + 5 * half],
                device_id=device, device_id_type=MESH,
            )

        part = pl.ds(4 * half, 4)
        lo, hi = low.at[n, part], high.at[n, part]
        if half == 0:
            lat_to, rim, rim_to, lo_to, hi_to = up, main.at[0:7], bot, cbr, cbl
        else:
            lat_to, rim, rim_to, lo_to, hi_to = dn, main.at[9:16], top, ctr, ctl
        beyond = [
            rc(0, rim, rim_to.at[n], (section, lat_to, lon)),
            rc(1, lo, lo_to.at[n], (section, lat_to, lt)),
            rc(2, hi, hi_to.at[n], (section, lat_to, rt)),
        ]
        across = [
            rc(3, lo, right.at[n, part], (section, lat, lt)),
            rc(4, hi, left.at[n, part], (section, lat, rt)),
        ]
        return beyond, across

    def start_halo(n, main, half):
        edge_columns(main, low.at[n], high.at[n], half)
        beyond, across = halo_copies(n, main, half)

        @pl.when(below if half else above)
        def _():
            for c in beyond:
                c.start()

        for c in across:
            c.start()

    def finish_halo(n, main):
        upward, across0 = halo_copies(n, main, 0)
        downward, across1 = halo_copies(n, main, 1)
        for c in across0 + across1:
            c.wait()

        @pl.when(above)
        def _():
            for c in upward:
                c.wait_send()
            for c in downward:
                c.wait_recv()

        @pl.when(below)
        def _():
            for c in downward:
                c.wait_send()
            for c in upward:
                c.wait_recv()

    def halo(n):
        return [r.at[n] for r in (top, bot, left, right, ctl, ctr, cbl, cbr)]

    greeted = 3 + jnp.where(above, 3, 0) + jnp.where(below, 3, 0)
    index_a = lax.rem(jnp.where(section == 1, plan[0], plan[3]), 2)
    loads_w[0].wait()
    for c in loads_x:
        c.wait()
    for half in range(2):
        stem_rows(x_ref, 1 - index_a, win, fx, main_b, half)
    pl.semaphore_wait(barrier, greeted)
    for half in range(2):
        start_halo(0, main_b, half)
    for half in range(2):
        stem_rows(x_ref, index_a, win, fx, send_a, half)
        copy_a(half).start()

    for n in range(2):

        @pl.when(jnp.logical_not(above))
        def _():
            for ref in (top, ctl, ctr):
                ref[n] = jnp.zeros(ref.shape[1:], BF)

        @pl.when(jnp.logical_not(below))
        def _():
            for ref in (bot, cbl, cbr):
                ref[n] = jnp.zeros(ref.shape[1:], BF)

    for ref in (f, fs, fp, fd, fl):
        rows = ref.shape[0]
        ref[:, 0:8] = jnp.zeros((rows, 8, 128), F32)
        ref[:, PADDED - 8 :] = jnp.zeros((rows, 8, 128), F32)
    for c in loads_w[1:]:
        c.wait()
    prepare_enc(wenc, we)
    prepare_down(wdown, wd)
    prepare_mid(wmid, wm)
    prepare_unite(wun, wu)

    finish_halo(0, main_b)
    widened(main_b, halo(0), f, ee, eb)
    copy_a(0).wait()
    start_halo(1, recv_a, 0)
    encoder(above, below, ee, eb, we, fs, fp, qc, qs, 14)
    deepen(above, below, qc, qs, wd, fd, dm, dc, dp, 3)
    copy_a(1).wait()
    start_halo(1, recv_a, 1)
    lift(above, below, dm, dc, dp, fd, wm, wup, fl, 5)
    join_operands(fs, fl, sc, sb, lc, lb)

    for half in range(2):
        merged_b[pl.ds(4 * half, 4)] = unite(sc, sb, lc, lb, wu, 4 * half, 4).reshape(4, WP, 256)
        copy_b(half).start()

    finish_halo(1, recv_a)
    widened(recv_a, halo(1), f, ee, eb)
    encoder(above, below, ee, eb, we, fs, fp, qc, qs, 14)
    deepen(above, below, qc, qs, wd, fd, dm, dc, dp, 3)
    lift(above, below, dm, dc, dp, fd, wm, wup, fl, 5)
    join_operands(fs, fl, sc, sb, lc, lb)
    merged_a[...] = unite(sc, sb, lc, lb, wu, 0, 8).reshape(8, WP, 256)
    store_a = pltpu.make_async_copy(merged_a, out_hbm.at[section], out_sem.at[0])
    store_a.start()

    for half in range(2):
        copy_b(half).wait()
    stays = jnp.where(section == 0, plan[1] < 2, plan[2] >= 2)

    def choose(i):
        merged_b[i] = jnp.where(stays, merged_b[i], recv_b[i])

    loop(HP, 4, choose)
    store_b = pltpu.make_async_copy(merged_b, out_hbm.at[1 - section], out_sem.at[1])
    store_b.start()
    store_a.wait()
    store_b.wait()


def project(m_hbm, wout_ref, out_hbm, m_ref, fo, buf, load_sems, sems):
    loads = [pltpu.make_async_copy(m_hbm.at[t], m_ref.at[t], load_sems.at[t]) for t in range(2)]
    for load in loads:
        load.start()
    w = nt(eye(VARS), wout_ref[...]).astype(BF)
    zero = jnp.zeros((VARS, C0), BF)
    both = jnp.concatenate(
        [jnp.concatenate([w, zero], axis=1), jnp.concatenate([zero, w], axis=1)], axis=0
    )
    i, j = grid_iota(256, 256)
    gather = one_hot((i // 64 % 2 == j // 128) & (j % 128 == 2 * (i % 64) + i // 128))
    copies = []
    for t in range(2):
        loads[t].wait()
        parts = []
        for p in range(0, HP, 2):
            m = [m_ref[t, p + k // 2][:, k % 2 * 128 : k % 2 * 128 + 128] for k in range(4)]
            u = nt(both, jnp.concatenate(m, axis=0)).astype(BF)
            for k in range(2):
                lanes = slice(k * 128, k * 128 + 128)
                parts.append(jnp.concatenate([u[:VARS, lanes], u[VARS:, lanes]], axis=1))
        v = nn(jnp.concatenate(parts, axis=0), gather)
        for h in range(H):
            rows = v[h // 2 * VARS : h // 2 * VARS + VARS]
            fo[t, pl.ds(h, VARS, stride=H), :] = rows[:, h % 2 * 128 : h % 2 * 128 + 128]
        buf[t] = fo[t].reshape(VARS, H, W).astype(BF)
        copy = pltpu.make_async_copy(buf.at[t], out_hbm.at[t], sems.at[t])
        copy.start()
        copies.append(copy)
    for copy in copies:
        copy.wait()


def shards(fields_in, plan, in_proj, enc_conv, down_conv, mid_conv, up_proj, unite_conv, out_proj):
    vmem = pl.BlockSpec(memory_space=pltpu.VMEM)
    hbm = pl.BlockSpec(memory_space=pltpu.HBM)
    dma = pltpu.SemaphoreType.DMA
    bf = lambda *s: pltpu.VMEM(s, BF)
    fl = lambda *s: pltpu.VMEM(s, F32)
    merged = pl.pallas_call(
        kernel,
        name="unet",
        out_shape=jax.ShapeDtypeStruct((2, HP, WP, 256), BF),
        in_specs=[pl.BlockSpec(memory_space=pltpu.SMEM)] + [hbm] * 7,
        out_specs=hbm,
        scratch_shapes=[
            bf(2, VARS, H, W), bf(C0, VARS), bf(9, C0, C0), bf(9, C0, C1), bf(9, C1, C1),
            bf(C0, C1), bf(9, C0, C1),
            fl(VARS * H, W),
            bf(H, WP, 128), bf(H, WP, 128), bf(H, WP, 128),
            bf(2, 8, 16, 128), bf(2, 8, 16, 128),
            bf(2, 7, WP, 128), bf(2, 7, WP, 128),
            bf(2, 8, 16, 128), bf(2, 8, 16, 128),
            bf(2, 4, 16, 128), bf(2, 4, 16, 128), bf(2, 4, 16, 128), bf(2, 4, 16, 128),
            fl(32, PADDED, 128), bf(2, 16, EXT, 128), bf(2, 16, EXT, 128),
            fl(28, PADDED, 128), fl(14, PADDED, 128), bf(2, 7, EXT, 128), bf(2, 7, EXT, 128),
            fl(12, PADDED, 128), bf(2, 6, EXT, 128), bf(2, 6, EXT, 128), bf(2, 6, EXT, 128),
            fl(10, PADDED, 128),
            bf(2, 10, WP, 128), bf(2, 10, WP, 128), bf(10, WP, 128), bf(10, WP, 128),
            bf(HP, WP, 256), bf(HP, WP, 256), bf(HP, WP, 256),
            bf(1024, 256), bf(1024, 256), bf(1536, 256), bf(2048, 256),
            dma((8,)), dma((6,)), dma((2,)), dma((2, 10)), dma((2, 10)), dma((2,)), dma((2,)), dma((2,)), dma((2,)),
        ],
        compiler_params=pltpu.CompilerParams(
            collective_id=0, has_side_effects=True, vmem_limit_bytes=61 * 2**20
        ),
    )(
        plan, fields_in, in_proj, enc_conv, jnp.swapaxes(down_conv, 1, 2),
        mid_conv, up_proj, unite_conv,
    )
    return pl.pallas_call(
        project,
        name="project",
        out_shape=jax.ShapeDtypeStruct((2, VARS, H, W), BF),
        in_specs=[hbm, vmem],
        out_specs=hbm,
        scratch_shapes=[
            bf(2, HP, WP, 256), fl(2, VARS * H, W), bf(2, VARS, H, W), dma((2,)), dma((2,)),
        ],
        compiler_params=pltpu.CompilerParams(vmem_limit_bytes=61 * 2**20),
    )(merged, out_proj.T)


def solution(mesh):
    return jax.shard_map(
        shards,
        mesh=mesh,
        in_specs=(P("section", None, "lat", "lon"), P(), P(), P(), P(), P(), P(), P(), P()),
        out_specs=P("section", None, "lat", "lon"),
        check_vma=False,
    )
```

```python
import functools

import jax
import jax.numpy as jnp
from jax import lax
from jax.experimental import pallas as pl
from jax.experimental.pallas import tpu as pltpu
from jax.sharding import PartitionSpec as P

F32, BF = jnp.float32, jnp.bfloat16
MESH = pl.DeviceIdType.MESH

VARS, C0, C1 = 96, 64, 128
COPIES = 8
H, W = 16, 128
HP, WP = H // 2, W // 2
EXT = WP + 16
PADDED = EXT + 16
MID = slice(8, 8 + EXT)
PREV = slice(7, 7 + EXT)
NEXT = slice(9, 9 + EXT)
OWN = slice(16, 16 + WP)
OWN_PREV = slice(15, 15 + WP)
OWN_NEXT = slice(17, 17 + WP)


def gelu(x):
    half = 0.5 * x
    inner = x * (0.7978845608028654 + 0.035677408136300125 * (x * x))
    return half + half * jnp.tanh(inner)


def rounded(x):
    return x.astype(BF).astype(F32)


def nn(a, b):
    return jnp.dot(a, b, preferred_element_type=F32)


def nt(a, b):
    return lax.dot_general(a, b, (((1,), (1,)), ((), ())), preferred_element_type=F32)


def grid_iota(rows, cols):
    shape = (rows, cols)
    return lax.broadcasted_iota(jnp.int32, shape, 0), lax.broadcasted_iota(jnp.int32, shape, 1)


def one_hot(mask):
    return jnp.where(mask, 1.0, 0.0).astype(BF)


def loop(count, step, body):
    def several(i, carry):
        for k in range(step):
            body(i * step + k)
        return carry

    if count == step:
        several(0, 0)
    else:
        lax.fori_loop(0, count // step, several, 0)


def eye(n):
    i, j = grid_iota(n, n)
    return one_hot(i == j)


def upper_lanes(rows):
    return lax.broadcasted_iota(jnp.int32, (rows, 128), 1) >= 64


def column_pairs(taps, channels):
    zero = jnp.zeros((C0, channels), BF)
    unit = eye(channels)
    out = []
    for a in range(3):
        b0, b1, b2 = taps[3 * a], taps[3 * a + 1], taps[3 * a + 2]
        stacked = jnp.concatenate([zero, b2, b1, b0, b2, b1, b0, zero], axis=0)
        out.append(nt(unit, stacked).astype(BF))
    return out


def fill_full_res(w_ref, base, blocks, rows):
    for k in range(4):
        for dr in range(2):
            a = k - dr
            lanes = slice(dr * 128, dr * 128 + 128)
            for at, col in ((0, 1), (64, 2), (512, 3), (576, 0)):
                where = base + at + k * 128
                if 0 <= a <= 2:
                    val = blocks[a][rows, col * 128 : col * 128 + 128]
                else:
                    val = jnp.zeros((64, 128), BF)
                w_ref[where : where + 64, lanes] = val


def prepare_enc(wenc, we):
    fill_full_res(we, 0, column_pairs(wenc, C0), slice(0, 64))


def prepare_down(wdown, wd):
    for k in range(4):
        for dr in range(2):
            a = k - dr
            for at, b in ((0, 0), (64, 2), (128, 1), (192, None)):
                where = k * 256 + at
                if b is not None and 0 <= a <= 2:
                    val = wdown[3 * a + b]
                else:
                    val = jnp.zeros((64, 128), BF)
                wd[where : where + 64, dr * 128 : dr * 128 + 128] = val


def prepare_mid(wmid, wm):
    taps = nt(eye(C1), wmid[...].reshape(9 * C1, C1)).astype(BF)
    for k in range(4):
        for dr in range(2):
            a = k - dr
            for b in range(3):
                where = k * 384 + b * 128
                if 0 <= a <= 2:
                    t = 3 * a + b
                    val = taps[:, t * 128 : t * 128 + 128]
                else:
                    val = jnp.zeros((128, 128), BF)
                wm[where : where + 128, dr * 128 : dr * 128 + 128] = val


def prepare_unite(wun, wu):
    blocks = column_pairs(wun, 2 * C0)
    fill_full_res(wu, 0, blocks, slice(64, 128))
    fill_full_res(wu, 1024, blocks, slice(0, 64))


def stem_rows(x_ref, index, win_ref, fx, dest, half):
    if half == 0:
        fx[...] = x_ref[index].astype(F32).reshape(VARS * H, W)
    i, j = grid_iota(128, 128)
    spread = one_hot(j == 2 * (i % 64) + i // 64)
    win = win_ref[...]
    hi = upper_lanes(WP)

    def body(g):
        first = 8 * half + 4 * g
        rows = [fx[pl.ds(first + k, VARS, stride=H), :].astype(BF) for k in range(4)]
        y = gelu(nn(win, jnp.concatenate(rows, axis=1))).astype(BF)
        stacked = jnp.concatenate([y[:, k * W : k * W + W] for k in range(4)], axis=0)
        z = nt(spread, stacked)
        for k in range(2):
            even = z[:WP, k * 128 : k * 128 + 128]
            odd = z[WP:, k * 128 : k * 128 + 128]
            at = first + 2 * k
            dest[at] = jnp.where(hi, pltpu.roll(odd, 64, 1), even).astype(BF)
            dest[at + 1] = jnp.where(hi, odd, pltpu.roll(even, 64, 1)).astype(BF)

    loop(2, 2, body)


def edge_columns(main, low, high, half):
    def body(k):
        q = 4 * half + k
        r0, r1 = main.at[2 * q], main.at[2 * q + 1]
        low[q] = jnp.concatenate(
            [r0[0:16].astype(F32)[0:8], r1[0:16].astype(F32)[0:8]], axis=0
        ).astype(BF)
        high[q] = jnp.concatenate(
            [r0[48:64].astype(F32)[8:16], r1[48:64].astype(F32)[8:16]], axis=0
        ).astype(BF)

    loop(4, 4, body)


def widened(main, halo, f, ee, eb):
    top, bot, left, right, ctl, ctr, cbl, cbr = halo

    def sides(q, at, lref, rref):
        lv, rv = lref[q].astype(F32), rref[q].astype(F32)
        f[at, 8:16] = lv[0:8]
        f[at + 1, 8:16] = lv[8:16]
        f[at, 80:88] = rv[0:8]
        f[at + 1, 80:88] = rv[8:16]

    def own(q):
        sides(q, 8 + 2 * q, left, right)
        f[8 + 2 * q, OWN] = main[2 * q].astype(F32)
        f[9 + 2 * q, OWN] = main[2 * q + 1].astype(F32)

    def corner(q):
        sides(q, 2 * q, ctl, ctr)
        sides(q, 24 + 2 * q, cbl, cbr)

    def rims(t):
        f[1 + t, OWN] = top[t].astype(F32)
        f[24 + t, OWN] = bot[t].astype(F32)

    loop(HP, 4, own)
    loop(4, 4, corner)
    loop(7, 7, rims)
    hi = upper_lanes(EXT)

    def split(q):
        for par in range(2):
            rr = 2 * q + par
            ee[par, q] = f[rr, MID].astype(BF)
            eb[par, q] = pltpu.roll(jnp.where(hi, f[rr, PREV], f[rr, NEXT]), 64, 1).astype(BF)

    loop(16, 4, split)


def quads(refs, first, count):
    pieces = []
    for ref in refs:
        for par, lag in ((1, 0), (0, 1), (1, 1), (0, 2)):
            v = ref[par, pl.ds(first + lag, count)]
            pieces.append(v.reshape(-1, v.shape[-1]))
    return jnp.concatenate(pieces, axis=1)


def kept(value, keep):
    return value if keep is None else jnp.where(keep, value, 0.0)


def inside(row, first, last, above, below):
    if isinstance(row, int):
        return above if row < first else below if row > last else None
    return ((row >= first) | above) & ((row <= last) | below)


def encoder(above, below, ee, eb, we, fs, fp, qc, qs, group):
    def body(g):
        first = g * group
        y = rounded(gelu(nn(quads((ee, eb), first, group), we[...])))
        for p in range(group):
            ii = first + p
            v = kept(y[p * EXT : p * EXT + EXT], inside(ii, 3, 10, above, below))
            v0, v1 = v[:, :128], v[:, 128:]
            fs[2 * ii, MID] = v0
            fs[2 * ii + 1, MID] = v1
            s = v0 + v1
            fp[ii, MID] = rounded((s + pltpu.roll(s, 64, 1)) * 0.25)

    loop(14 // group, 1, body)
    hi = upper_lanes(EXT)

    def split(q):
        for par in range(2):
            ii = 2 * q + par
            qc[par, q] = fp[ii, MID].astype(BF)
            qs[par, q] = jnp.where(hi, fp[ii, NEXT], fp[ii, PREV]).astype(BF)

    loop(7, 7, split)


def row_quads(refs, first, count):
    pieces = []
    for lag in range(2):
        for par in range(2):
            for ref in refs:
                v = ref[par, pl.ds(first + lag, count)]
                pieces.append(v.reshape(-1, v.shape[-1]))
    return jnp.concatenate(pieces, axis=1)


def deepen(above, below, qc, qs, wd, fd, dm, dc, dp, group_d):
    def down(g):
        first = g * group_d
        y = rounded(gelu(nn(row_quads((qs, qc), first, group_d), wd[...])))
        for p in range(group_d):
            k = first + p
            v = kept(y[p * EXT : p * EXT + EXT], inside(k, 1, 4, above, below))
            fd[2 * k, MID] = v[:, :128]
            fd[2 * k + 1, MID] = v[:, 128:]

    loop(6 // group_d, 1, down)

    def split(q):
        for par in range(2):
            dd = 2 * q + par
            dm[par, q] = fd[dd, PREV].astype(BF)
            dc[par, q] = fd[dd, MID].astype(BF)
            dp[par, q] = fd[dd, NEXT].astype(BF)

    loop(6, 3, split)


def lift(above, below, dm, dc, dp, fd, wm, wup_ref, fl, group_m):
    up = jnp.concatenate([wup_ref[...], wup_ref[...]], axis=0)

    def mid(g):
        first = g * group_m
        y = gelu(nn(row_quads((dm, dc, dp), first, group_m), wm[...]))
        rows = []
        for p in range(group_m):
            k = first + p
            for dr in range(2):
                v = y[p * EXT : p * EXT + EXT, dr * 128 : dr * 128 + 128]
                keep = inside(2 * k + dr, 1, 8, above, below)
                rows.append(kept(v + fd[2 * k + 1 + dr, MID], keep).astype(BF))
        z = rounded(nt(jnp.concatenate(rows, axis=0), up))
        for p in range(group_m):
            k = first + p
            for dr in range(2):
                at = (2 * p + dr) * EXT
                fl[2 * k + dr, MID] = z[at : at + EXT]

    loop(5 // group_m, 1, mid)


def join_operands(fs, fl, sc, sb, lc, lb):
    hi = upper_lanes(WP)

    def skip(q):
        for par in range(2):
            idx = 2 * (q + 2) + par
            sc[par, q] = fs[idx, OWN].astype(BF)
            sb[par, q] = pltpu.roll(
                jnp.where(hi, fs[idx, OWN_PREV], fs[idx, OWN_NEXT]), 64, 1
            ).astype(BF)

    loop(10, 5, skip)

    def lift(m):
        lc[m] = fl[m, OWN].astype(BF)
        lb[m] = jnp.where(hi, fl[m, OWN_NEXT], fl[m, OWN_PREV]).astype(BF)

    loop(10, 10, lift)


def unite(sc, sb, lc, lb, wu, first, group):
    pieces = [quads((sc, sb), first, group)]
    for ref in (lc, lb):
        for lag in (0, 1, 1, 2):
            pieces.append(ref[pl.ds(first + lag, group)].reshape(-1, 128))
    return gelu(nn(jnp.concatenate(pieces, axis=1), wu[...])).astype(BF)


def project_weights(wout_ref, both, gather):
    w = nt(eye(VARS), wout_ref[...]).astype(BF)
    zero = jnp.zeros((VARS, C0), BF)
    both[...] = jnp.concatenate(
        [jnp.concatenate([w, zero], axis=1), jnp.concatenate([zero, w], axis=1)], axis=0
    )
    i, j = grid_iota(256, 256)
    gather[...] = one_hot((i // 64 % 2 == j // 128) & (j % 128 == 2 * (i % 64) + i // 128))


def project(m_ref, both, gather, fo, out):
    parts = []
    for p in range(0, HP, 2):
        m = [m_ref[p + k // 2][:, k % 2 * 128 : k % 2 * 128 + 128] for k in range(4)]
        u = nt(both[...], jnp.concatenate(m, axis=0)).astype(BF)
        for k in range(2):
            lanes = slice(k * 128, k * 128 + 128)
            parts.append(jnp.concatenate([u[:VARS, lanes], u[VARS:, lanes]], axis=1))
    v = nn(jnp.concatenate(parts, axis=0), gather[...])
    for h in range(H):
        rows = v[h // 2 * VARS : h // 2 * VARS + VARS]
        fo[pl.ds(h, VARS, stride=H), :] = rows[:, h % 2 * 128 : h % 2 * 128 + 128]
    out[...] = fo[...].reshape(VARS, H, W).astype(BF)


def kernel(
    plan, x_hbm, win_hbm, wenc_hbm, wdown_hbm, wmid_hbm, wup_hbm, wun_hbm, wout_hbm, out_ref,
    x_ref, win, wenc, wdown, wmid, wup, wun, wout,
    fx, send_a, main_b, recv_a, low, high, top, bot, left, right, ctl, ctr, cbl, cbr,
    f, ee, eb, fs, fp, qc, qs, fd, dm, dc, dp, fl, sc, sb, lc, lb,
    merged_a, merged_b, recv_b, we, wd, wm, wu, both, gather,
    x_sem, w_sem, halo_send, halo_recv, a_send, a_recv, b_send, b_recv,
):
    section, lat, lon = lax.axis_index("section"), lax.axis_index("lat"), lax.axis_index("lon")
    lats, lons = lax.axis_size("lat"), lax.axis_size("lon")
    above, below = lat > 0, lat < lats - 1
    up, dn = jnp.maximum(lat - 1, 0), jnp.minimum(lat + 1, lats - 1)
    lt, rt = lax.rem(lon + lons - 1, lons), lax.rem(lon + 1, lons)
    partner = (1 - section, lat, lon)

    loads_w = [
        pltpu.make_async_copy(src, dst, w_sem.at[n])
        for n, (src, dst) in enumerate(
            (
                (win_hbm, win),
                (wenc_hbm, wenc),
                (wdown_hbm, wdown),
                (wmid_hbm, wmid),
                (wup_hbm, wup),
                (wun_hbm, wun),
                (wout_hbm, wout),
            )
        )
    ]
    loads_x = [
        pltpu.make_async_copy(
            x_hbm.at[n // 4, pl.ds(n % 4 * 24, 24)],
            x_ref.at[n // 4, pl.ds(n % 4 * 24, 24)],
            x_sem.at[n],
        )
        for n in range(8)
    ]
    barrier = pltpu.get_barrier_semaphore()

    def greet(device):
        pl.semaphore_signal(barrier, inc=1, device_id=device, device_id_type=MESH)

    greet(partner)
    greet((section, lat, lt))
    greet((section, lat, rt))

    @pl.when(above)
    def _():
        for c in (lt, lon, rt):
            greet((section, up, c))

    @pl.when(below)
    def _():
        for c in (lt, lon, rt):
            greet((section, dn, c))

    loads_w[0].start()
    for c in loads_x:
        c.start()
    for c in loads_w[1:]:
        c.start()

    def copy_a(half):
        rows = pl.ds(8 * half, 8)
        return pltpu.make_async_remote_copy(
            src_ref=send_a.at[rows], dst_ref=recv_a.at[rows],
            send_sem=a_send.at[half], recv_sem=a_recv.at[half],
            device_id=partner, device_id_type=MESH,
        )

    def copy_b(half):
        rows = pl.ds(4 * half, 4)
        return pltpu.make_async_remote_copy(
            src_ref=merged_b.at[rows], dst_ref=recv_b.at[rows],
            send_sem=b_send.at[half], recv_sem=b_recv.at[half],
            device_id=partner, device_id_type=MESH,
        )

    def halo_copies(n, main, half):
        def rc(d, src, dst, device):
            return pltpu.make_async_remote_copy(
                src_ref=src, dst_ref=dst,
                send_sem=halo_send.at[n, d + 5 * half], recv_sem=halo_recv.at[n, d + 5 * half],
                device_id=device, device_id_type=MESH,
            )

        part = pl.ds(4 * half, 4)
        lo, hi = low.at[n, part], high.at[n, part]
        if half == 0:
            lat_to, rim, rim_to, lo_to, hi_to = up, main.at[0:7], bot, cbr, cbl
        else:
            lat_to, rim, rim_to, lo_to, hi_to = dn, main.at[9:16], top, ctr, ctl
        beyond = [
            rc(0, rim, rim_to.at[n], (section, lat_to, lon)),
            rc(1, lo, lo_to.at[n], (section, lat_to, lt)),
            rc(2, hi, hi_to.at[n], (section, lat_to, rt)),
        ]
        across = [
            rc(3, lo, right.at[n, part], (section, lat, lt)),
            rc(4, hi, left.at[n, part], (section, lat, rt)),
        ]
        return beyond, across

    def start_halo(n, main, half):
        edge_columns(main, low.at[n], high.at[n], half)
        beyond, across = halo_copies(n, main, half)

        @pl.when(below if half else above)
        def _():
            for c in beyond:
                c.start()

        for c in across:
            c.start()

    def finish_halo(n, main):
        upward, across0 = halo_copies(n, main, 0)
        downward, across1 = halo_copies(n, main, 1)
        for c in across0 + across1:
            c.wait()

        @pl.when(above)
        def _():
            for c in upward:
                c.wait_send()
            for c in downward:
                c.wait_recv()

        @pl.when(below)
        def _():
            for c in downward:
                c.wait_send()
            for c in upward:
                c.wait_recv()

    def halo(n):
        return [r.at[n] for r in (top, bot, left, right, ctl, ctr, cbl, cbr)]

    greeted = 3 + jnp.where(above, 3, 0) + jnp.where(below, 3, 0)
    index_a = lax.rem(jnp.where(section == 1, plan[0], plan[3]), 2)
    loads_w[0].wait()
    for c in loads_x:
        c.wait()
    for half in range(2):
        stem_rows(x_ref, index_a, win, fx, send_a, half)
    for half in range(2):
        stem_rows(x_ref, 1 - index_a, win, fx, main_b, half)
    pl.semaphore_wait(barrier, greeted)
    for half in range(2):
        copy_a(half).start()
        start_halo(0, main_b, half)

    for n in range(2):

        @pl.when(jnp.logical_not(above))
        def _():
            for ref in (top, ctl, ctr):
                ref[n] = jnp.zeros(ref.shape[1:], BF)

        @pl.when(jnp.logical_not(below))
        def _():
            for ref in (bot, cbl, cbr):
                ref[n] = jnp.zeros(ref.shape[1:], BF)

    for ref in (f, fs, fp, fd, fl):
        rows = ref.shape[0]
        ref[:, 0:8] = jnp.zeros((rows, 8, 128), F32)
        ref[:, PADDED - 8 :] = jnp.zeros((rows, 8, 128), F32)
    for c in loads_w[1:]:
        c.wait()
    prepare_enc(wenc, we)
    prepare_down(wdown, wd)
    prepare_mid(wmid, wm)
    prepare_unite(wun, wu)
    project_weights(wout, both, gather)

    finish_halo(0, main_b)
    widened(main_b, halo(0), f, ee, eb)
    copy_a(0).wait()
    start_halo(1, recv_a, 0)
    encoder(above, below, ee, eb, we, fs, fp, qc, qs, 14)
    copy_a(1).wait()
    start_halo(1, recv_a, 1)
    deepen(above, below, qc, qs, wd, fd, dm, dc, dp, 3)
    lift(above, below, dm, dc, dp, fd, wm, wup, fl, 5)
    join_operands(fs, fl, sc, sb, lc, lb)

    for half in range(2):
        merged_b[pl.ds(4 * half, 4)] = unite(sc, sb, lc, lb, wu, 4 * half, 4).reshape(4, WP, 256)
        copy_b(half).start()

    finish_halo(1, recv_a)
    widened(recv_a, halo(1), f, ee, eb)
    encoder(above, below, ee, eb, we, fs, fp, qc, qs, 14)
    deepen(above, below, qc, qs, wd, fd, dm, dc, dp, 3)
    lift(above, below, dm, dc, dp, fd, wm, wup, fl, 5)
    join_operands(fs, fl, sc, sb, lc, lb)
    def unite_a(g):
        merged_a[pl.ds(4 * g, 4)] = unite(sc, sb, lc, lb, wu, 4 * g, 4).reshape(4, WP, 256)

    loop(2, 1, unite_a)
    project(merged_a, both, gather, fx, out_ref.at[section])

    for half in range(2):
        copy_b(half).wait()
    stays = jnp.where(section == 0, plan[1] < 2, plan[2] >= 2)

    def choose(i):
        merged_b[i] = jnp.where(stays, merged_b[i], recv_b[i])

    loop(HP, 4, choose)
    project(merged_b, both, gather, fx, out_ref.at[1 - section])


def hand_over(src, dst, buf, load_sems, store_sems):
    rows = 2 * VARS // COPIES
    parts = [(n * rows // VARS, pl.ds(n * rows % VARS, rows)) for n in range(COPIES)]
    loads = [
        pltpu.make_async_copy(src.at[p], buf.at[p], load_sems.at[n]) for n, p in enumerate(parts)
    ]
    stores = [
        pltpu.make_async_copy(buf.at[p], dst.at[p], store_sems.at[n]) for n, p in enumerate(parts)
    ]
    for c in loads:
        c.start()
    for load, store in zip(loads, stores):
        load.wait()
        store.start()
    for c in stores:
        c.wait()


def shards(fields_in, plan, in_proj, enc_conv, down_conv, mid_conv, up_proj, unite_conv, out_proj):
    hbm = pl.BlockSpec(memory_space=pltpu.HBM)
    dma = pltpu.SemaphoreType.DMA
    bf = lambda *s: pltpu.VMEM(s, BF)
    fl = lambda *s: pltpu.VMEM(s, F32)
    return pl.pallas_call(
        kernel,
        name="unet",
        out_shape=pltpu.VMEM((2, VARS, H, W), BF),
        in_specs=[pl.BlockSpec(memory_space=pltpu.SMEM)] + [hbm] * 8,
        out_specs=pl.BlockSpec(memory_space=pltpu.VMEM),
        scratch_shapes=[
            bf(2, VARS, H, W), bf(C0, VARS), bf(9, C0, C0), bf(9, C0, C1), bf(9, C1, C1),
            bf(C0, C1), bf(9, C0, C1), bf(C0, VARS),
            fl(VARS * H, W),
            bf(H, WP, 128), bf(H, WP, 128), bf(H, WP, 128),
            bf(2, 8, 16, 128), bf(2, 8, 16, 128),
            bf(2, 7, WP, 128), bf(2, 7, WP, 128),
            bf(2, 8, 16, 128), bf(2, 8, 16, 128),
            bf(2, 4, 16, 128), bf(2, 4, 16, 128), bf(2, 4, 16, 128), bf(2, 4, 16, 128),
            fl(32, PADDED, 128), bf(2, 16, EXT, 128), bf(2, 16, EXT, 128),
            fl(28, PADDED, 128), fl(14, PADDED, 128), bf(2, 7, EXT, 128), bf(2, 7, EXT, 128),
            fl(12, PADDED, 128), bf(2, 6, EXT, 128), bf(2, 6, EXT, 128), bf(2, 6, EXT, 128),
            fl(10, PADDED, 128),
            bf(2, 10, WP, 128), bf(2, 10, WP, 128), bf(10, WP, 128), bf(10, WP, 128),
            bf(HP, WP, 256), bf(HP, WP, 256), bf(HP, WP, 256),
            bf(1024, 256), bf(1024, 256), bf(1536, 256), bf(2048, 256), bf(2 * VARS, 128), bf(256, 256),
            dma((8,)), dma((7,)), dma((2, 10)), dma((2, 10)), dma((2,)), dma((2,)), dma((2,)), dma((2,)),
        ],
        compiler_params=pltpu.CompilerParams(
            collective_id=0, has_side_effects=True, vmem_limit_bytes=61 * 2**20
        ),
    )(
        plan, fields_in, in_proj, enc_conv, jnp.swapaxes(down_conv, 1, 2),
        mid_conv, up_proj, unite_conv, out_proj.T,
    )

def solution(mesh):
    return jax.shard_map(
        shards,
        mesh=mesh,
        in_specs=(P("section", None, "lat", "lon"), P(), P(), P(), P(), P(), P(), P(), P()),
        out_specs=P("section", None, "lat", "lon"),
        check_vma=False,
    )
```

```python
import functools

import jax
import jax.numpy as jnp
from jax import lax
from jax.experimental import pallas as pl
from jax.experimental.pallas import tpu as pltpu
from jax.sharding import PartitionSpec as P

F32, BF = jnp.float32, jnp.bfloat16
MESH = pl.DeviceIdType.MESH

VARS, C0, C1 = 96, 64, 128
COPIES = 8
H, W = 16, 128
HP, WP = H // 2, W // 2
EXT = WP + 16
PADDED = EXT + 16
MID = slice(8, 8 + EXT)
PREV = slice(7, 7 + EXT)
NEXT = slice(9, 9 + EXT)
OWN = slice(16, 16 + WP)
OWN_PREV = slice(15, 15 + WP)
OWN_NEXT = slice(17, 17 + WP)


def gelu(x):
    half = 0.5 * x
    inner = x * (0.7978845608028654 + 0.035677408136300125 * (x * x))
    return half + half * jnp.tanh(inner)


def rounded(x):
    return x.astype(BF).astype(F32)


def nn(a, b):
    return jnp.dot(a, b, preferred_element_type=F32)


def nt(a, b):
    return lax.dot_general(a, b, (((1,), (1,)), ((), ())), preferred_element_type=F32)


def grid_iota(rows, cols):
    shape = (rows, cols)
    return lax.broadcasted_iota(jnp.int32, shape, 0), lax.broadcasted_iota(jnp.int32, shape, 1)


def one_hot(mask):
    return jnp.where(mask, 1.0, 0.0).astype(BF)


def loop(count, step, body):
    def several(i, carry):
        for k in range(step):
            body(i * step + k)
        return carry

    if count == step:
        several(0, 0)
    else:
        lax.fori_loop(0, count // step, several, 0)


def eye(n):
    i, j = grid_iota(n, n)
    return one_hot(i == j)


def upper_lanes(rows):
    return lax.broadcasted_iota(jnp.int32, (rows, 128), 1) >= 64


def column_pairs(taps, channels):
    zero = jnp.zeros((C0, channels), BF)
    unit = eye(channels)
    out = []
    for a in range(3):
        b0, b1, b2 = taps[3 * a], taps[3 * a + 1], taps[3 * a + 2]
        stacked = jnp.concatenate([zero, b2, b1, b0, b2, b1, b0, zero], axis=0)
        out.append(nt(unit, stacked).astype(BF))
    return out


def fill_full_res(w_ref, base, blocks, rows):
    for k in range(4):
        for dr in range(2):
            a = k - dr
            lanes = slice(dr * 128, dr * 128 + 128)
            for at, col in ((0, 1), (64, 2), (512, 3), (576, 0)):
                where = base + at + k * 128
                if 0 <= a <= 2:
                    val = blocks[a][rows, col * 128 : col * 128 + 128]
                else:
                    val = jnp.zeros((64, 128), BF)
                w_ref[where : where + 64, lanes] = val


def prepare_enc(wenc, we):
    fill_full_res(we, 0, column_pairs(wenc, C0), slice(0, 64))


def prepare_down(wdown, wd):
    for k in range(4):
        for dr in range(2):
            a = k - dr
            for at, b in ((0, 0), (64, 2), (128, 1), (192, None)):
                where = k * 256 + at
                if b is not None and 0 <= a <= 2:
                    val = wdown[3 * a + b]
                else:
                    val = jnp.zeros((64, 128), BF)
                wd[where : where + 64, dr * 128 : dr * 128 + 128] = val


def prepare_mid(wmid, wm):
    taps = nt(eye(C1), wmid[...].reshape(9 * C1, C1)).astype(BF)
    for k in range(4):
        for dr in range(2):
            a = k - dr
            for b in range(3):
                where = k * 384 + b * 128
                if 0 <= a <= 2:
                    t = 3 * a + b
                    val = taps[:, t * 128 : t * 128 + 128]
                else:
                    val = jnp.zeros((128, 128), BF)
                wm[where : where + 128, dr * 128 : dr * 128 + 128] = val


def prepare_unite(wun, wu):
    blocks = column_pairs(wun, 2 * C0)
    fill_full_res(wu, 0, blocks, slice(64, 128))
    fill_full_res(wu, 1024, blocks, slice(0, 64))


def stem_rows(x_ref, index, win_ref, fx, dest, half):
    if half == 0:
        fx[...] = x_ref[index].astype(F32).reshape(VARS * H, W)
    i, j = grid_iota(128, 128)
    spread = one_hot(j == 2 * (i % 64) + i // 64)
    win = win_ref[...]
    hi = upper_lanes(WP)

    def body(g):
        first = 8 * half + 4 * g
        rows = [fx[pl.ds(first + k, VARS, stride=H), :].astype(BF) for k in range(4)]
        y = gelu(nn(win, jnp.concatenate(rows, axis=1))).astype(BF)
        stacked = jnp.concatenate([y[:, k * W : k * W + W] for k in range(4)], axis=0)
        z = nt(spread, stacked)
        for k in range(2):
            even = z[:WP, k * 128 : k * 128 + 128]
            odd = z[WP:, k * 128 : k * 128 + 128]
            at = first + 2 * k
            dest[at] = jnp.where(hi, pltpu.roll(odd, 64, 1), even).astype(BF)
            dest[at + 1] = jnp.where(hi, odd, pltpu.roll(even, 64, 1)).astype(BF)

    loop(2, 2, body)


def edge_columns(main, low, high, half):
    def body(k):
        q = 4 * half + k
        r0, r1 = main.at[2 * q], main.at[2 * q + 1]
        low[q] = jnp.concatenate(
            [r0[0:16].astype(F32)[0:8], r1[0:16].astype(F32)[0:8]], axis=0
        ).astype(BF)
        high[q] = jnp.concatenate(
            [r0[48:64].astype(F32)[8:16], r1[48:64].astype(F32)[8:16]], axis=0
        ).astype(BF)

    loop(4, 4, body)


def widened(main, halo, f, ee, eb):
    top, bot, left, right, ctl, ctr, cbl, cbr = halo

    def sides(q, at, lref, rref):
        lv, rv = lref[q].astype(F32), rref[q].astype(F32)
        f[at, 8:16] = lv[0:8]
        f[at + 1, 8:16] = lv[8:16]
        f[at, 80:88] = rv[0:8]
        f[at + 1, 80:88] = rv[8:16]

    def own(q):
        sides(q, 8 + 2 * q, left, right)
        f[8 + 2 * q, OWN] = main[2 * q].astype(F32)
        f[9 + 2 * q, OWN] = main[2 * q + 1].astype(F32)

    def corner(q):
        sides(q, 2 * q, ctl, ctr)
        sides(q, 24 + 2 * q, cbl, cbr)

    def rims(t):
        f[1 + t, OWN] = top[t].astype(F32)
        f[24 + t, OWN] = bot[t].astype(F32)

    loop(HP, 8, own)
    loop(4, 4, corner)
    loop(7, 7, rims)
    hi = upper_lanes(EXT)

    def split(q):
        for par in range(2):
            rr = 2 * q + par
            ee[par, q] = f[rr, MID].astype(BF)
            eb[par, q] = pltpu.roll(jnp.where(hi, f[rr, PREV], f[rr, NEXT]), 64, 1).astype(BF)

    loop(16, 8, split)


def quads(refs, first, count):
    pieces = []
    for ref in refs:
        for par, lag in ((1, 0), (0, 1), (1, 1), (0, 2)):
            v = ref[par, pl.ds(first + lag, count)]
            pieces.append(v.reshape(-1, v.shape[-1]))
    return jnp.concatenate(pieces, axis=1)


def kept(value, keep):
    return value if keep is None else jnp.where(keep, value, 0.0)


def inside(row, first, last, above, below):
    if isinstance(row, int):
        return above if row < first else below if row > last else None
    return ((row >= first) | above) & ((row <= last) | below)


def encoder(above, below, ee, eb, we, fs, fp, qc, qs, group):
    def body(g):
        first = g * group
        y = rounded(gelu(nn(quads((ee, eb), first, group), we[...])))
        for p in range(group):
            ii = first + p
            v = kept(y[p * EXT : p * EXT + EXT], inside(ii, 3, 10, above, below))
            v0, v1 = v[:, :128], v[:, 128:]
            fs[2 * ii, MID] = v0
            fs[2 * ii + 1, MID] = v1
            s = v0 + v1
            fp[ii, MID] = rounded((s + pltpu.roll(s, 64, 1)) * 0.25)

    loop(14 // group, 1, body)
    hi = upper_lanes(EXT)

    def split(q):
        for par in range(2):
            ii = 2 * q + par
            qc[par, q] = fp[ii, MID].astype(BF)
            qs[par, q] = jnp.where(hi, fp[ii, NEXT], fp[ii, PREV]).astype(BF)

    loop(7, 7, split)


def row_quads(refs, first, count):
    pieces = []
    for lag in range(2):
        for par in range(2):
            for ref in refs:
                v = ref[par, pl.ds(first + lag, count)]
                pieces.append(v.reshape(-1, v.shape[-1]))
    return jnp.concatenate(pieces, axis=1)


def deepen(above, below, qc, qs, wd, fd, dm, dc, dp, group_d):
    def down(g):
        first = g * group_d
        y = rounded(gelu(nn(row_quads((qs, qc), first, group_d), wd[...])))
        for p in range(group_d):
            k = first + p
            v = kept(y[p * EXT : p * EXT + EXT], inside(k, 1, 4, above, below))
            fd[2 * k, MID] = v[:, :128]
            fd[2 * k + 1, MID] = v[:, 128:]

    loop(6 // group_d, 1, down)

    def split(q):
        for par in range(2):
            dd = 2 * q + par
            dm[par, q] = fd[dd, PREV].astype(BF)
            dc[par, q] = fd[dd, MID].astype(BF)
            dp[par, q] = fd[dd, NEXT].astype(BF)

    loop(6, 6, split)


def lift(above, below, dm, dc, dp, fd, wm, wup_ref, fl, group_m):
    up = jnp.concatenate([wup_ref[...], wup_ref[...]], axis=0)

    def mid(g):
        first = g * group_m
        y = gelu(nn(row_quads((dm, dc, dp), first, group_m), wm[...]))
        rows = []
        for p in range(group_m):
            k = first + p
            for dr in range(2):
                v = y[p * EXT : p * EXT + EXT, dr * 128 : dr * 128 + 128]
                keep = inside(2 * k + dr, 1, 8, above, below)
                rows.append(kept(v + fd[2 * k + 1 + dr, MID], keep).astype(BF))
        z = rounded(nt(jnp.concatenate(rows, axis=0), up))
        for p in range(group_m):
            k = first + p
            for dr in range(2):
                at = (2 * p + dr) * EXT
                fl[2 * k + dr, MID] = z[at : at + EXT]

    loop(5 // group_m, 1, mid)


def join_operands(fs, fl, sc, sb, lc, lb):
    hi = upper_lanes(WP)

    def skip(q):
        for par in range(2):
            idx = 2 * (q + 2) + par
            sc[par, q] = fs[idx, OWN].astype(BF)
            sb[par, q] = pltpu.roll(
                jnp.where(hi, fs[idx, OWN_PREV], fs[idx, OWN_NEXT]), 64, 1
            ).astype(BF)

    loop(10, 10, skip)

    def lift(m):
        lc[m] = fl[m, OWN].astype(BF)
        lb[m] = jnp.where(hi, fl[m, OWN_NEXT], fl[m, OWN_PREV]).astype(BF)

    loop(10, 10, lift)


def unite(sc, sb, lc, lb, wu, first, group):
    pieces = [quads((sc, sb), first, group)]
    for ref in (lc, lb):
        for lag in (0, 1, 1, 2):
            pieces.append(ref[pl.ds(first + lag, group)].reshape(-1, 128))
    return gelu(nn(jnp.concatenate(pieces, axis=1), wu[...])).astype(BF)


def project_weights(wout_ref, both, gather):
    w = nt(eye(VARS), wout_ref[...]).astype(BF)
    zero = jnp.zeros((VARS, C0), BF)
    both[...] = jnp.concatenate(
        [jnp.concatenate([w, zero], axis=1), jnp.concatenate([zero, w], axis=1)], axis=0
    )
    i, j = grid_iota(256, 256)
    gather[...] = one_hot((i // 64 % 2 == j // 128) & (j % 128 == 2 * (i % 64) + i // 128))


def project(m_ref, both, gather, fo, out):
    parts = []
    for p in range(0, HP, 2):
        m = [m_ref[p + k // 2][:, k % 2 * 128 : k % 2 * 128 + 128] for k in range(4)]
        u = nt(both[...], jnp.concatenate(m, axis=0)).astype(BF)
        for k in range(2):
            lanes = slice(k * 128, k * 128 + 128)
            parts.append(jnp.concatenate([u[:VARS, lanes], u[VARS:, lanes]], axis=1))
    v = nn(jnp.concatenate(parts, axis=0), gather[...])
    for h in range(H):
        rows = v[h // 2 * VARS : h // 2 * VARS + VARS]
        fo[pl.ds(h, VARS, stride=H), :] = rows[:, h % 2 * 128 : h % 2 * 128 + 128]
    out[...] = fo[...].reshape(VARS, H, W).astype(BF)


def kernel(
    plan, x_hbm, win_hbm, wenc_hbm, wdown_hbm, wmid_hbm, wup_hbm, wun_hbm, wout_hbm, out_ref,
    x_ref, win, wenc, wdown, wmid, wup, wun, wout,
    fx, send_a, main_b, recv_a, low, high, top, bot, left, right, ctl, ctr, cbl, cbr,
    f, ee, eb, fs, fp, qc, qs, fd, dm, dc, dp, fl, sc, sb, lc, lb,
    merged, merged_b, recv_b, we, wd, wm, wu, both, gather,
    x_sem, w_sem, halo_send, halo_recv, a_send, a_recv, b_send, b_recv,
):
    section, lat, lon = lax.axis_index("section"), lax.axis_index("lat"), lax.axis_index("lon")
    lats, lons = lax.axis_size("lat"), lax.axis_size("lon")
    above, below = lat > 0, lat < lats - 1
    up, dn = jnp.maximum(lat - 1, 0), jnp.minimum(lat + 1, lats - 1)
    lt, rt = lax.rem(lon + lons - 1, lons), lax.rem(lon + 1, lons)
    partner = (1 - section, lat, lon)

    loads_w = [
        pltpu.make_async_copy(src, dst, w_sem.at[n])
        for n, (src, dst) in enumerate(
            (
                (win_hbm, win),
                (wenc_hbm, wenc),
                (wdown_hbm, wdown),
                (wmid_hbm, wmid),
                (wup_hbm, wup),
                (wun_hbm, wun),
                (wout_hbm, wout),
            )
        )
    ]
    loads_x = [
        pltpu.make_async_copy(
            x_hbm.at[n // 4, pl.ds(n % 4 * 24, 24)],
            x_ref.at[n // 4, pl.ds(n % 4 * 24, 24)],
            x_sem.at[n],
        )
        for n in range(8)
    ]
    barrier = pltpu.get_barrier_semaphore()

    def greet(device):
        pl.semaphore_signal(barrier, inc=1, device_id=device, device_id_type=MESH)

    greet(partner)
    greet((section, lat, lt))
    greet((section, lat, rt))

    @pl.when(above)
    def _():
        for c in (lt, lon, rt):
            greet((section, up, c))

    @pl.when(below)
    def _():
        for c in (lt, lon, rt):
            greet((section, dn, c))

    loads_w[0].start()
    for c in loads_x:
        c.start()
    for c in loads_w[1:]:
        c.start()

    def copy_a(half):
        rows = pl.ds(8 * half, 8)
        return pltpu.make_async_remote_copy(
            src_ref=send_a.at[rows], dst_ref=recv_a.at[rows],
            send_sem=a_send.at[half], recv_sem=a_recv.at[half],
            device_id=partner, device_id_type=MESH,
        )

    def copy_b(half):
        rows = pl.ds(4 * half, 4)
        return pltpu.make_async_remote_copy(
            src_ref=merged_b.at[rows], dst_ref=recv_b.at[rows],
            send_sem=b_send.at[half], recv_sem=b_recv.at[half],
            device_id=partner, device_id_type=MESH,
        )

    def halo_copies(n, main, half):
        def rc(d, src, dst, device):
            return pltpu.make_async_remote_copy(
                src_ref=src, dst_ref=dst,
                send_sem=halo_send.at[n, d + 5 * half], recv_sem=halo_recv.at[n, d + 5 * half],
                device_id=device, device_id_type=MESH,
            )

        part = pl.ds(4 * half, 4)
        lo, hi = low.at[n, part], high.at[n, part]
        if half == 0:
            lat_to, rim, rim_to, lo_to, hi_to = up, main.at[0:7], bot, cbr, cbl
        else:
            lat_to, rim, rim_to, lo_to, hi_to = dn, main.at[9:16], top, ctr, ctl
        beyond = [
            rc(0, rim, rim_to.at[n], (section, lat_to, lon)),
            rc(1, lo, lo_to.at[n], (section, lat_to, lt)),
            rc(2, hi, hi_to.at[n], (section, lat_to, rt)),
        ]
        across = [
            rc(3, lo, right.at[n, part], (section, lat, lt)),
            rc(4, hi, left.at[n, part], (section, lat, rt)),
        ]
        return beyond, across

    def start_halo(n, main, half):
        edge_columns(main, low.at[n], high.at[n], half)
        beyond, across = halo_copies(n, main, half)

        @pl.when(below if half else above)
        def _():
            for c in beyond:
                c.start()

        for c in across:
            c.start()

    def finish_halo(n, main):
        upward, across0 = halo_copies(n, main, 0)
        downward, across1 = halo_copies(n, main, 1)
        for c in across0 + across1:
            c.wait()

        @pl.when(above)
        def _():
            for c in upward:
                c.wait_send()
            for c in downward:
                c.wait_recv()

        @pl.when(below)
        def _():
            for c in downward:
                c.wait_send()
            for c in upward:
                c.wait_recv()

    def halo(n):
        return [r.at[n] for r in (top, bot, left, right, ctl, ctr, cbl, cbr)]

    greeted = 3 + jnp.where(above, 3, 0) + jnp.where(below, 3, 0)
    index_a = lax.rem(jnp.where(section == 1, plan[0], plan[3]), 2)
    loads_w[0].wait()
    for c in loads_x:
        c.wait()
    for half in range(2):
        stem_rows(x_ref, index_a, win, fx, send_a, half)
    for half in range(2):
        stem_rows(x_ref, 1 - index_a, win, fx, main_b, half)
    pl.semaphore_wait(barrier, greeted)
    for half in range(2):
        copy_a(half).start()
        start_halo(0, main_b, half)

    for n in range(2):

        @pl.when(jnp.logical_not(above))
        def _():
            for ref in (top, ctl, ctr):
                ref[n] = jnp.zeros(ref.shape[1:], BF)

        @pl.when(jnp.logical_not(below))
        def _():
            for ref in (bot, cbl, cbr):
                ref[n] = jnp.zeros(ref.shape[1:], BF)

    for ref in (f, fs, fp, fd, fl):
        rows = ref.shape[0]
        ref[:, 0:8] = jnp.zeros((rows, 8, 128), F32)
        ref[:, PADDED - 8 :] = jnp.zeros((rows, 8, 128), F32)
    for c in loads_w[1:]:
        c.wait()
    prepare_enc(wenc, we)
    prepare_down(wdown, wd)
    prepare_mid(wmid, wm)
    prepare_unite(wun, wu)
    project_weights(wout, both, gather)

    finish_halo(0, main_b)
    widened(main_b, halo(0), f, ee, eb)
    copy_a(0).wait()
    start_halo(1, recv_a, 0)
    encoder(above, below, ee, eb, we, fs, fp, qc, qs, 14)
    copy_a(1).wait()
    start_halo(1, recv_a, 1)
    deepen(above, below, qc, qs, wd, fd, dm, dc, dp, 3)
    lift(above, below, dm, dc, dp, fd, wm, wup, fl, 5)
    join_operands(fs, fl, sc, sb, lc, lb)

    for half in range(2):
        merged_b[pl.ds(4 * half, 4)] = unite(sc, sb, lc, lb, wu, 4 * half, 4).reshape(4, WP, 256)
        copy_b(half).start()

    finish_halo(1, recv_a)
    widened(recv_a, halo(1), f, ee, eb)
    encoder(above, below, ee, eb, we, fs, fp, qc, qs, 14)
    deepen(above, below, qc, qs, wd, fd, dm, dc, dp, 3)
    lift(above, below, dm, dc, dp, fd, wm, wup, fl, 5)
    join_operands(fs, fl, sc, sb, lc, lb)
    def unite_a(g):
        merged[0, pl.ds(4 * g, 4)] = unite(sc, sb, lc, lb, wu, 4 * g, 4).reshape(4, WP, 256)

    loop(2, 1, unite_a)

    for half in range(2):
        copy_b(half).wait()
    stays = jnp.where(section == 0, plan[1] < 2, plan[2] >= 2)

    def choose(i):
        merged[1, i] = jnp.where(stays, merged_b[i], recv_b[i])

    loop(HP, 8, choose)

    def finish(n):
        turn = section + n * (1 - 2 * section)
        project(merged.at[n], both, gather, fx, out_ref.at[turn])

    loop(2, 1, finish)


def shards(fields_in, plan, in_proj, enc_conv, down_conv, mid_conv, up_proj, unite_conv, out_proj):
    hbm = pl.BlockSpec(memory_space=pltpu.HBM)
    dma = pltpu.SemaphoreType.DMA
    bf = lambda *s: pltpu.VMEM(s, BF)
    fl = lambda *s: pltpu.VMEM(s, F32)
    return pl.pallas_call(
        kernel,
        name="unet",
        out_shape=pltpu.VMEM((2, VARS, H, W), BF),
        in_specs=[pl.BlockSpec(memory_space=pltpu.SMEM)] + [hbm] * 8,
        out_specs=pl.BlockSpec(memory_space=pltpu.VMEM),
        scratch_shapes=[
            bf(2, VARS, H, W), bf(C0, VARS), bf(9, C0, C0), bf(9, C0, C1), bf(9, C1, C1),
            bf(C0, C1), bf(9, C0, C1), bf(C0, VARS),
            fl(VARS * H, W),
            bf(H, WP, 128), bf(H, WP, 128), bf(H, WP, 128),
            bf(2, 8, 16, 128), bf(2, 8, 16, 128),
            bf(2, 7, WP, 128), bf(2, 7, WP, 128),
            bf(2, 8, 16, 128), bf(2, 8, 16, 128),
            bf(2, 4, 16, 128), bf(2, 4, 16, 128), bf(2, 4, 16, 128), bf(2, 4, 16, 128),
            fl(32, PADDED, 128), bf(2, 16, EXT, 128), bf(2, 16, EXT, 128),
            fl(28, PADDED, 128), fl(14, PADDED, 128), bf(2, 7, EXT, 128), bf(2, 7, EXT, 128),
            fl(12, PADDED, 128), bf(2, 6, EXT, 128), bf(2, 6, EXT, 128), bf(2, 6, EXT, 128),
            fl(10, PADDED, 128),
            bf(2, 10, WP, 128), bf(2, 10, WP, 128), bf(10, WP, 128), bf(10, WP, 128),
            bf(2, HP, WP, 256), bf(HP, WP, 256), bf(HP, WP, 256),
            bf(1024, 256), bf(1024, 256), bf(1536, 256), bf(2048, 256), bf(2 * VARS, 128), bf(256, 256),
            dma((8,)), dma((7,)), dma((2, 10)), dma((2, 10)), dma((2,)), dma((2,)), dma((2,)), dma((2,)),
        ],
        compiler_params=pltpu.CompilerParams(
            collective_id=0, has_side_effects=True, vmem_limit_bytes=61 * 2**20
        ),
    )(
        plan, fields_in, in_proj, enc_conv, jnp.swapaxes(down_conv, 1, 2),
        mid_conv, up_proj, unite_conv, out_proj.T,
    )

def solution(mesh):
    return jax.shard_map(
        shards,
        mesh=mesh,
        in_specs=(P("section", None, "lat", "lon"), P(), P(), P(), P(), P(), P(), P(), P()),
        out_specs=P("section", None, "lat", "lon"),
        check_vma=False,
    )
```

```python
import functools

import jax
import jax.numpy as jnp
from jax import lax
from jax.experimental import pallas as pl
from jax.experimental.pallas import tpu as pltpu
from jax.sharding import PartitionSpec as P

F32, BF = jnp.float32, jnp.bfloat16
MESH = pl.DeviceIdType.MESH

VARS, C0, C1 = 96, 64, 128
COPIES = 8
H, W = 16, 128
HP, WP = H // 2, W // 2
EXT = WP + 16
PADDED = EXT + 16
MID = slice(8, 8 + EXT)
PREV = slice(7, 7 + EXT)
NEXT = slice(9, 9 + EXT)
OWN = slice(16, 16 + WP)
OWN_PREV = slice(15, 15 + WP)
OWN_NEXT = slice(17, 17 + WP)


def gelu(x):
    half = 0.5 * x
    inner = x * (0.7978845608028654 + 0.035677408136300125 * (x * x))
    return half + half * jnp.tanh(inner)


def rounded(x):
    return x.astype(BF).astype(F32)


def nn(a, b):
    return jnp.dot(a, b, preferred_element_type=F32)


def nt(a, b):
    return lax.dot_general(a, b, (((1,), (1,)), ((), ())), preferred_element_type=F32)


def grid_iota(rows, cols):
    shape = (rows, cols)
    return lax.broadcasted_iota(jnp.int32, shape, 0), lax.broadcasted_iota(jnp.int32, shape, 1)


def one_hot(mask):
    return jnp.where(mask, 1.0, 0.0).astype(BF)


def loop(count, step, body):
    def several(i, carry):
        for k in range(step):
            body(i * step + k)
        return carry

    if count == step:
        several(0, 0)
    else:
        lax.fori_loop(0, count // step, several, 0)


def eye(n):
    i, j = grid_iota(n, n)
    return one_hot(i == j)


def upper_lanes(rows):
    return lax.broadcasted_iota(jnp.int32, (rows, 128), 1) >= 64


def column_pairs(taps, channels):
    zero = jnp.zeros((C0, channels), BF)
    unit = eye(channels)
    out = []
    for a in range(3):
        b0, b1, b2 = taps[3 * a], taps[3 * a + 1], taps[3 * a + 2]
        stacked = jnp.concatenate([zero, b2, b1, b0, b2, b1, b0, zero], axis=0)
        out.append(nt(unit, stacked).astype(BF))
    return out


def fill_full_res(w_ref, base, blocks, rows):
    for k in range(4):
        for dr in range(2):
            a = k - dr
            lanes = slice(dr * 128, dr * 128 + 128)
            for at, col in ((0, 1), (64, 2), (512, 3), (576, 0)):
                where = base + at + k * 128
                if 0 <= a <= 2:
                    val = blocks[a][rows, col * 128 : col * 128 + 128]
                else:
                    val = jnp.zeros((64, 128), BF)
                w_ref[where : where + 64, lanes] = val


def prepare_enc(wenc, we):
    fill_full_res(we, 0, column_pairs(wenc, C0), slice(0, 64))


def prepare_down(wdown, wd):
    for k in range(4):
        for dr in range(2):
            a = k - dr
            for at, b in ((0, 0), (64, 2), (128, 1), (192, None)):
                where = k * 256 + at
                if b is not None and 0 <= a <= 2:
                    val = wdown[3 * a + b]
                else:
                    val = jnp.zeros((64, 128), BF)
                wd[where : where + 64, dr * 128 : dr * 128 + 128] = val


def prepare_mid(wmid, wm):
    taps = nt(eye(C1), wmid[...].reshape(9 * C1, C1)).astype(BF)
    for k in range(4):
        for dr in range(2):
            a = k - dr
            for b in range(3):
                where = k * 384 + b * 128
                if 0 <= a <= 2:
                    t = 3 * a + b
                    val = taps[:, t * 128 : t * 128 + 128]
                else:
                    val = jnp.zeros((128, 128), BF)
                wm[where : where + 128, dr * 128 : dr * 128 + 128] = val


def prepare_unite(wun, wu):
    blocks = column_pairs(wun, 2 * C0)
    fill_full_res(wu, 0, blocks, slice(64, 128))
    fill_full_res(wu, 1024, blocks, slice(0, 64))


def stem_rows(x_ref, index, win_ref, fx, dest, half):
    if half == 0:
        fx[...] = x_ref[index].astype(F32).reshape(VARS * H, W)
    i, j = grid_iota(128, 128)
    spread = one_hot(j == 2 * (i % 64) + i // 64)
    win = win_ref[...]
    hi = upper_lanes(WP)

    def body(g):
        first = 8 * half + 4 * g
        rows = [fx[pl.ds(first + k, VARS, stride=H), :].astype(BF) for k in range(4)]
        y = gelu(nn(win, jnp.concatenate(rows, axis=1))).astype(BF)
        stacked = jnp.concatenate([y[:, k * W : k * W + W] for k in range(4)], axis=0)
        z = nt(spread, stacked)
        for k in range(2):
            even = z[:WP, k * 128 : k * 128 + 128]
            odd = z[WP:, k * 128 : k * 128 + 128]
            at = first + 2 * k
            dest[at] = jnp.where(hi, pltpu.roll(odd, 64, 1), even).astype(BF)
            dest[at + 1] = jnp.where(hi, odd, pltpu.roll(even, 64, 1)).astype(BF)

    loop(2, 2, body)


def edge_columns(main, low, high, half):
    def body(k):
        q = 4 * half + k
        r0, r1 = main.at[2 * q], main.at[2 * q + 1]
        low[q] = jnp.concatenate(
            [r0[0:16].astype(F32)[0:8], r1[0:16].astype(F32)[0:8]], axis=0
        ).astype(BF)
        high[q] = jnp.concatenate(
            [r0[48:64].astype(F32)[8:16], r1[48:64].astype(F32)[8:16]], axis=0
        ).astype(BF)

    loop(4, 4, body)


def operands(f, ee, eb, q, first, count):
    hi = upper_lanes(count)
    at = slice(first, first + count)
    for par in range(2):
        row = f.at[2 * q + par]
        prev, this, after = (row[8 + first + d : 8 + first + d + count] for d in (-1, 0, 1))
        ee[par, q, at] = this.astype(BF)
        eb[par, q, at] = pltpu.roll(jnp.where(hi, prev, after), 64, 1).astype(BF)


def widen_inner(main, f, ee, eb):
    for q in range(HP):
        f[8 + 2 * q, OWN] = main[2 * q].astype(F32)
        f[9 + 2 * q, OWN] = main[2 * q + 1].astype(F32)
        operands(f, ee, eb, 4 + q, 16, EXT - 32)


def widen_outer(halo, f, ee, eb):
    top, bot, left, right, ctl, ctr, cbl, cbr = halo

    def sides(q, at, lref, rref):
        lv, rv = lref[q].astype(F32), rref[q].astype(F32)
        f[at, 8:16] = lv[0:8]
        f[at + 1, 8:16] = lv[8:16]
        f[at, 80:88] = rv[0:8]
        f[at + 1, 80:88] = rv[8:16]

    for q in range(HP):
        sides(q, 8 + 2 * q, left, right)
    for q in range(4):
        sides(q, 2 * q, ctl, ctr)
        sides(q, 24 + 2 * q, cbl, cbr)
    for t in range(7):
        f[1 + t, OWN] = top[t].astype(F32)
        f[24 + t, OWN] = bot[t].astype(F32)
    for q in range(HP):
        operands(f, ee, eb, 4 + q, 0, 16)
        operands(f, ee, eb, 4 + q, EXT - 16, 16)
    for q in (0, 1, 2, 3, 12, 13, 14, 15):
        operands(f, ee, eb, q, 0, EXT)


def quads(refs, first, count):
    pieces = []
    for ref in refs:
        for par, lag in ((1, 0), (0, 1), (1, 1), (0, 2)):
            v = ref[par, pl.ds(first + lag, count)]
            pieces.append(v.reshape(-1, v.shape[-1]))
    return jnp.concatenate(pieces, axis=1)


def kept(value, keep):
    return value if keep is None else jnp.where(keep, value, 0.0)


def inside(row, first, last, above, below):
    if isinstance(row, int):
        return above if row < first else below if row > last else None
    return ((row >= first) | above) & ((row <= last) | below)


def encoder(above, below, ee, eb, we, fs, fp, qc, qs, group):
    def body(g):
        first = g * group
        y = rounded(gelu(nn(quads((ee, eb), first, group), we[...])))
        for p in range(group):
            ii = first + p
            v = kept(y[p * EXT : p * EXT + EXT], inside(ii, 3, 10, above, below))
            v0, v1 = v[:, :128], v[:, 128:]
            fs[2 * ii, MID] = v0
            fs[2 * ii + 1, MID] = v1
            s = v0 + v1
            fp[ii, MID] = rounded((s + pltpu.roll(s, 64, 1)) * 0.25)

    loop(14 // group, 1, body)
    hi = upper_lanes(EXT)

    def split(q):
        for par in range(2):
            ii = 2 * q + par
            qc[par, q] = fp[ii, MID].astype(BF)
            qs[par, q] = jnp.where(hi, fp[ii, NEXT], fp[ii, PREV]).astype(BF)

    loop(7, 7, split)


def row_quads(refs, first, count):
    pieces = []
    for lag in range(2):
        for par in range(2):
            for ref in refs:
                v = ref[par, pl.ds(first + lag, count)]
                pieces.append(v.reshape(-1, v.shape[-1]))
    return jnp.concatenate(pieces, axis=1)


def deepen(above, below, qc, qs, wd, fd, dm, dc, dp, group_d):
    def down(g):
        first = g * group_d
        y = rounded(gelu(nn(row_quads((qs, qc), first, group_d), wd[...])))
        for p in range(group_d):
            k = first + p
            v = kept(y[p * EXT : p * EXT + EXT], inside(k, 1, 4, above, below))
            fd[2 * k, MID] = v[:, :128]
            fd[2 * k + 1, MID] = v[:, 128:]

    loop(6 // group_d, 1, down)

    def split(q):
        for par in range(2):
            dd = 2 * q + par
            dm[par, q] = fd[dd, PREV].astype(BF)
            dc[par, q] = fd[dd, MID].astype(BF)
            dp[par, q] = fd[dd, NEXT].astype(BF)

    loop(6, 6, split)


def lift(above, below, dm, dc, dp, fd, wm, wup_ref, fl, group_m):
    up = jnp.concatenate([wup_ref[...], wup_ref[...]], axis=0)

    def mid(g):
        first = g * group_m
        y = gelu(nn(row_quads((dm, dc, dp), first, group_m), wm[...]))
        rows = []
        for p in range(group_m):
            k = first + p
            for dr in range(2):
                v = y[p * EXT : p * EXT + EXT, dr * 128 : dr * 128 + 128]
                keep = inside(2 * k + dr, 1, 8, above, below)
                rows.append(kept(v + fd[2 * k + 1 + dr, MID], keep).astype(BF))
        z = rounded(nt(jnp.concatenate(rows, axis=0), up))
        for p in range(group_m):
            k = first + p
            for dr in range(2):
                at = (2 * p + dr) * EXT
                fl[2 * k + dr, MID] = z[at : at + EXT]

    loop(5 // group_m, 1, mid)


def join_operands(fs, fl, sc, sb, lc, lb):
    hi = upper_lanes(WP)

    def skip(q):
        for par in range(2):
            idx = 2 * (q + 2) + par
            sc[par, q] = fs[idx, OWN].astype(BF)
            sb[par, q] = pltpu.roll(
                jnp.where(hi, fs[idx, OWN_PREV], fs[idx, OWN_NEXT]), 64, 1
            ).astype(BF)

    loop(10, 10, skip)

    def lift(m):
        lc[m] = fl[m, OWN].astype(BF)
        lb[m] = jnp.where(hi, fl[m, OWN_NEXT], fl[m, OWN_PREV]).astype(BF)

    loop(10, 10, lift)


def unite(sc, sb, lc, lb, wu, first, group):
    pieces = [quads((sc, sb), first, group)]
    for ref in (lc, lb):
        for lag in (0, 1, 1, 2):
            pieces.append(ref[pl.ds(first + lag, group)].reshape(-1, 128))
    return gelu(nn(jnp.concatenate(pieces, axis=1), wu[...])).astype(BF)


def project_weights(wout_ref, both, gather):
    w = nt(eye(VARS), wout_ref[...]).astype(BF)
    zero = jnp.zeros((VARS, C0), BF)
    both[...] = jnp.concatenate(
        [jnp.concatenate([w, zero], axis=1), jnp.concatenate([zero, w], axis=1)], axis=0
    )
    i, j = grid_iota(256, 256)
    gather[...] = one_hot((i // 64 % 2 == j // 128) & (j % 128 == 2 * (i % 64) + i // 128))


def project(m_ref, both, gather, fo, out):
    parts = []
    for p in range(0, HP, 2):
        m = [m_ref[p + k // 2][:, k % 2 * 128 : k % 2 * 128 + 128] for k in range(4)]
        u = nt(both[...], jnp.concatenate(m, axis=0)).astype(BF)
        for k in range(2):
            lanes = slice(k * 128, k * 128 + 128)
            parts.append(jnp.concatenate([u[:VARS, lanes], u[VARS:, lanes]], axis=1))
    v = nn(jnp.concatenate(parts, axis=0), gather[...])
    for h in range(H):
        rows = v[h // 2 * VARS : h // 2 * VARS + VARS]
        fo[pl.ds(h, VARS, stride=H), :] = rows[:, h % 2 * 128 : h % 2 * 128 + 128]
    out[...] = fo[...].reshape(VARS, H, W).astype(BF)


def kernel(
    plan, x_hbm, win_hbm, wenc_hbm, wdown_hbm, wmid_hbm, wup_hbm, wun_hbm, wout_hbm, out_ref,
    x_ref, win, wenc, wdown, wmid, wup, wun, wout,
    fx, send_a, main_b, recv_a, low, high, top, bot, left, right, ctl, ctr, cbl, cbr,
    f, ee, eb, fs, fp, qc, qs, fd, dm, dc, dp, fl, sc, sb, lc, lb,
    merged, merged_b, recv_b, we, wd, wm, wu, both, gather,
    x_sem, w_sem, halo_send, halo_recv, a_send, a_recv, b_send, b_recv,
):
    section, lat, lon = lax.axis_index("section"), lax.axis_index("lat"), lax.axis_index("lon")
    lats, lons = lax.axis_size("lat"), lax.axis_size("lon")
    above, below = lat > 0, lat < lats - 1
    up, dn = jnp.maximum(lat - 1, 0), jnp.minimum(lat + 1, lats - 1)
    lt, rt = lax.rem(lon + lons - 1, lons), lax.rem(lon + 1, lons)
    partner = (1 - section, lat, lon)

    loads_w = [
        pltpu.make_async_copy(src, dst, w_sem.at[n])
        for n, (src, dst) in enumerate(
            (
                (win_hbm, win),
                (wenc_hbm, wenc),
                (wdown_hbm, wdown),
                (wmid_hbm, wmid),
                (wup_hbm, wup),
                (wun_hbm, wun),
                (wout_hbm, wout),
            )
        )
    ]
    loads_x = [
        pltpu.make_async_copy(
            x_hbm.at[n // 4, pl.ds(n % 4 * 24, 24)],
            x_ref.at[n // 4, pl.ds(n % 4 * 24, 24)],
            x_sem.at[n],
        )
        for n in range(8)
    ]
    barrier = pltpu.get_barrier_semaphore()

    def greet(device):
        pl.semaphore_signal(barrier, inc=1, device_id=device, device_id_type=MESH)

    greet(partner)
    greet((section, lat, lt))
    greet((section, lat, rt))

    @pl.when(above)
    def _():
        for c in (lt, lon, rt):
            greet((section, up, c))

    @pl.when(below)
    def _():
        for c in (lt, lon, rt):
            greet((section, dn, c))

    loads_w[0].start()
    for c in loads_x:
        c.start()
    for c in loads_w[1:]:
        c.start()

    def copy_a(half):
        rows = pl.ds(8 * half, 8)
        return pltpu.make_async_remote_copy(
            src_ref=send_a.at[rows], dst_ref=recv_a.at[rows],
            send_sem=a_send.at[half], recv_sem=a_recv.at[half],
            device_id=partner, device_id_type=MESH,
        )

    def copy_b(half):
        rows = pl.ds(4 * half, 4)
        return pltpu.make_async_remote_copy(
            src_ref=merged_b.at[rows], dst_ref=recv_b.at[rows],
            send_sem=b_send.at[half], recv_sem=b_recv.at[half],
            device_id=partner, device_id_type=MESH,
        )

    def halo_copies(n, main, half):
        def rc(d, src, dst, device):
            return pltpu.make_async_remote_copy(
                src_ref=src, dst_ref=dst,
                send_sem=halo_send.at[n, d + 5 * half], recv_sem=halo_recv.at[n, d + 5 * half],
                device_id=device, device_id_type=MESH,
            )

        part = pl.ds(4 * half, 4)
        lo, hi = low.at[n, part], high.at[n, part]
        if half == 0:
            lat_to, rim, rim_to, lo_to, hi_to = up, main.at[0:7], bot, cbr, cbl
        else:
            lat_to, rim, rim_to, lo_to, hi_to = dn, main.at[9:16], top, ctr, ctl
        beyond = [
            rc(0, rim, rim_to.at[n], (section, lat_to, lon)),
            rc(1, lo, lo_to.at[n], (section, lat_to, lt)),
            rc(2, hi, hi_to.at[n], (section, lat_to, rt)),
        ]
        across = [
            rc(3, lo, right.at[n, part], (section, lat, lt)),
            rc(4, hi, left.at[n, part], (section, lat, rt)),
        ]
        return beyond, across

    def start_halo(n, main, half):
        edge_columns(main, low.at[n], high.at[n], half)
        beyond, across = halo_copies(n, main, half)

        @pl.when(below if half else above)
        def _():
            for c in beyond:
                c.start()

        for c in across:
            c.start()

    def finish_halo(n, main):
        upward, across0 = halo_copies(n, main, 0)
        downward, across1 = halo_copies(n, main, 1)
        for c in across0 + across1:
            c.wait()

        @pl.when(above)
        def _():
            for c in upward:
                c.wait_send()
            for c in downward:
                c.wait_recv()

        @pl.when(below)
        def _():
            for c in downward:
                c.wait_send()
            for c in upward:
                c.wait_recv()

    def halo(n):
        return [r.at[n] for r in (top, bot, left, right, ctl, ctr, cbl, cbr)]

    greeted = 3 + jnp.where(above, 3, 0) + jnp.where(below, 3, 0)
    index_a = lax.rem(jnp.where(section == 1, plan[0], plan[3]), 2)
    loads_w[0].wait()
    for c in loads_x:
        c.wait()
    for half in range(2):
        stem_rows(x_ref, index_a, win, fx, send_a, half)
    for half in range(2):
        stem_rows(x_ref, 1 - index_a, win, fx, main_b, half)
    pl.semaphore_wait(barrier, greeted)
    for half in range(2):
        copy_a(half).start()
        start_halo(0, main_b, half)

    for n in range(2):

        @pl.when(jnp.logical_not(above))
        def _():
            for ref in (top, ctl, ctr):
                ref[n] = jnp.zeros(ref.shape[1:], BF)

        @pl.when(jnp.logical_not(below))
        def _():
            for ref in (bot, cbl, cbr):
                ref[n] = jnp.zeros(ref.shape[1:], BF)

    for ref in (f, fs, fp, fd, fl):
        rows = ref.shape[0]
        ref[:, 0:8] = jnp.zeros((rows, 8, 128), F32)
        ref[:, PADDED - 8 :] = jnp.zeros((rows, 8, 128), F32)
    for c in loads_w[1:]:
        c.wait()
    prepare_enc(wenc, we)
    prepare_down(wdown, wd)
    prepare_mid(wmid, wm)
    prepare_unite(wun, wu)
    project_weights(wout, both, gather)

    widen_inner(main_b, f, ee, eb)
    finish_halo(0, main_b)
    widen_outer(halo(0), f, ee, eb)
    copy_a(0).wait()
    start_halo(1, recv_a, 0)
    encoder(above, below, ee, eb, we, fs, fp, qc, qs, 14)
    copy_a(1).wait()
    start_halo(1, recv_a, 1)
    deepen(above, below, qc, qs, wd, fd, dm, dc, dp, 3)
    lift(above, below, dm, dc, dp, fd, wm, wup, fl, 5)
    join_operands(fs, fl, sc, sb, lc, lb)

    for half in range(2):
        merged_b[pl.ds(4 * half, 4)] = unite(sc, sb, lc, lb, wu, 4 * half, 4).reshape(4, WP, 256)
        copy_b(half).start()

    widen_inner(recv_a, f, ee, eb)
    finish_halo(1, recv_a)
    widen_outer(halo(1), f, ee, eb)
    encoder(above, below, ee, eb, we, fs, fp, qc, qs, 14)
    deepen(above, below, qc, qs, wd, fd, dm, dc, dp, 3)
    lift(above, below, dm, dc, dp, fd, wm, wup, fl, 5)
    join_operands(fs, fl, sc, sb, lc, lb)
    def unite_a(g):
        merged[0, pl.ds(4 * g, 4)] = unite(sc, sb, lc, lb, wu, 4 * g, 4).reshape(4, WP, 256)

    loop(2, 1, unite_a)

    for half in range(2):
        copy_b(half).wait()
    stays = jnp.where(section == 0, plan[1] < 2, plan[2] >= 2)

    def choose(i):
        merged[1, i] = jnp.where(stays, merged_b[i], recv_b[i])

    loop(HP, 8, choose)

    def finish(n):
        turn = section + n * (1 - 2 * section)
        project(merged.at[n], both, gather, fx, out_ref.at[turn])

    loop(2, 1, finish)


def shards(fields_in, plan, in_proj, enc_conv, down_conv, mid_conv, up_proj, unite_conv, out_proj):
    hbm = pl.BlockSpec(memory_space=pltpu.HBM)
    dma = pltpu.SemaphoreType.DMA
    bf = lambda *s: pltpu.VMEM(s, BF)
    fl = lambda *s: pltpu.VMEM(s, F32)
    return pl.pallas_call(
        kernel,
        name="unet",
        out_shape=pltpu.VMEM((2, VARS, H, W), BF),
        in_specs=[pl.BlockSpec(memory_space=pltpu.SMEM)] + [hbm] * 8,
        out_specs=pl.BlockSpec(memory_space=pltpu.VMEM),
        scratch_shapes=[
            bf(2, VARS, H, W), bf(C0, VARS), bf(9, C0, C0), bf(9, C0, C1), bf(9, C1, C1),
            bf(C0, C1), bf(9, C0, C1), bf(C0, VARS),
            fl(VARS * H, W),
            bf(H, WP, 128), bf(H, WP, 128), bf(H, WP, 128),
            bf(2, 8, 16, 128), bf(2, 8, 16, 128),
            bf(2, 7, WP, 128), bf(2, 7, WP, 128),
            bf(2, 8, 16, 128), bf(2, 8, 16, 128),
            bf(2, 4, 16, 128), bf(2, 4, 16, 128), bf(2, 4, 16, 128), bf(2, 4, 16, 128),
            fl(32, PADDED, 128), bf(2, 16, EXT, 128), bf(2, 16, EXT, 128),
            fl(28, PADDED, 128), fl(14, PADDED, 128), bf(2, 7, EXT, 128), bf(2, 7, EXT, 128),
            fl(12, PADDED, 128), bf(2, 6, EXT, 128), bf(2, 6, EXT, 128), bf(2, 6, EXT, 128),
            fl(10, PADDED, 128),
            bf(2, 10, WP, 128), bf(2, 10, WP, 128), bf(10, WP, 128), bf(10, WP, 128),
            bf(2, HP, WP, 256), bf(HP, WP, 256), bf(HP, WP, 256),
            bf(1024, 256), bf(1024, 256), bf(1536, 256), bf(2048, 256), bf(2 * VARS, 128), bf(256, 256),
            dma((8,)), dma((7,)), dma((2, 10)), dma((2, 10)), dma((2,)), dma((2,)), dma((2,)), dma((2,)),
        ],
        compiler_params=pltpu.CompilerParams(
            collective_id=0, has_side_effects=True, vmem_limit_bytes=61 * 2**20
        ),
    )(
        plan, fields_in, in_proj, enc_conv, jnp.swapaxes(down_conv, 1, 2),
        mid_conv, up_proj, unite_conv, out_proj.T,
    )

def solution(mesh):
    return jax.shard_map(
        shards,
        mesh=mesh,
        in_specs=(P("section", None, "lat", "lon"), P(), P(), P(), P(), P(), P(), P(), P()),
        out_specs=P("section", None, "lat", "lon"),
        check_vma=False,
    )
```
